256 devices in a mesh: tok: 64 (over y, z, core), head: 4 (over x).
Axes of the slice: x: 4, y: 4, z: 8, core: 2. Of those that a mesh axis runs over, the one named last changes fastest.
Arguments:
- tokens: bfloat16 [16384, 1024], P('tok'), may hold values from -6 to 6
- gain_one: float32 [1024], replicated, may hold values from 0.5 to 1.5
- qkv_one: bfloat16 [3, 1024, 1024], P(None, None, 'head'), may hold values from -0.1875 to 0.1875
- out_one: bfloat16 [1024, 1024], P('head'), may hold values from -0.1875 to 0.1875
- gain_two: float32 [1024], replicated, may hold values from 0.5 to 1.5
- qkv_two: bfloat16 [3, 1024, 1024], P(None, None, 'head'), may hold values from -0.1875 to 0.1875
- out_two: bfloat16 [1024, 1024], P('head'), may hold values from -0.1875 to 0.1875
- hilbert_pos: int32 [16384], replicated, may hold values from 0 to 16383, as said below
- scene: int32 [16384], replicated, may hold values from 0 to 127, never falling along the last dimension, each value on 1 to 256 neighbouring positions
- cotangent: bfloat16 [16384, 1024], P('tok'), may hold values from -16 to 16
Outputs:
- grad_input: bfloat16 [16384, 1024], P('tok')
- qkv_grad_one: float32 [3, 1024, 1024], P(None, 'tok', 'head')
- out_grad_one: float32 [1024, 1024], P('tok', 'head')
- gain_grad_one: float32 [1024], P('tok')
- qkv_grad_two: float32 [3, 1024, 1024], P(None, 'tok', 'head')
- out_grad_two: float32 [1024, 1024], P('tok', 'head')
- gain_grad_two: float32 [1024], P('tok')
The draws below stay inside these ranges and needn't reach their ends.
Inputs may be any that keep to these rules, and one draw needn't show every extreme that they name: `hilbert_pos`: A permutation. Of the 256 Z positions k * 256 to (k + 1) * 256 - 1, at most 8 have Hilbert positions in one block m * 256 to (m + 1) * 256 - 1, and in every draw some pair of blocks reaches 8.
All inputs are finite; a program needn't handle non-finite values.
Results may differ from the reference program's by a relative error of at most 0.023.
Values may be sent and summed in bfloat16 or wider, within the bound.
A program may use at most 64 MiB of HBM per device.

```python
import math
import jax
import jax.numpy as jnp
import numpy as np
from jax import lax

D = 1024
HEADS = 16
HEAD_DIM = 64
WINDOW = 512
TOK_DEV = 256
TOKENS = 16384


def draw_hilbert_pos(key, part):
    dev_count = TOKENS // TOK_DEV
    mean_len = TOK_DEV // dev_count
    subkeys = jax.random.split(key, 5)
    pair_count = dev_count // 2
    spread = jax.random.randint(subkeys[0], (pair_count,), 0, mean_len + 1)
    spread = spread.at[0].set(mean_len)
    piece_len = jnp.concatenate([mean_len + spread, mean_len - spread])
    piece_len = piece_len[jax.random.permutation(subkeys[1], dev_count)]
    piece_end = jnp.cumsum(piece_len)
    rank_ids = jnp.arange(TOK_DEV, dtype=jnp.int32)
    piece_of = jnp.sum((rank_ids[:, None] >= piece_end[None, :]).astype(jnp.int32), axis=1)
    device_order = jax.random.permutation(subkeys[2], dev_count).astype(jnp.int32)
    device_place = jnp.argsort(device_order).astype(jnp.int32)
    sources = jnp.arange(dev_count, dtype=jnp.int32)
    targets = device_order[(device_place[:, None] + piece_of[None, :]) % dev_count]
    send_perm = jax.vmap(lambda subkey: jax.random.permutation(subkey, TOK_DEV))(jax.random.split(subkeys[3], dev_count)).astype(jnp.int32)
    recv_perm = jax.vmap(lambda subkey: jax.random.permutation(subkey, TOK_DEV))(jax.random.split(subkeys[4], dev_count)).astype(jnp.int32)
    z_index = sources[:, None] * TOK_DEV + send_perm
    h_index = targets * TOK_DEV + recv_perm[targets, rank_ids[None, :]]
    result = jnp.zeros((TOKENS,), jnp.int32).at[z_index.reshape(-1)].set(h_index.reshape(-1))
    return result


def strengthened(drawn, key, source, target, blocks, factor):
    owner, partner = [(jnp.arange(drawn.shape[position]) // (drawn.shape[position] // blocks)).reshape([-1 if axis == position else 1 for axis in range(drawn.ndim)]) for position in (source, target)]
    chosen = jax.random.permutation(key, blocks)[partner]
    strong = (owner == chosen) | (owner == (partner + blocks // 2) % blocks)
    return jnp.where(strong, factor * drawn, drawn)


def levels(stream_key, extent, cuts, least, largest):
    factor_of = 1.0
    for position, shards_of in cuts:
        steps = jax.random.uniform(jax.random.fold_in(jax.random.fold_in(stream_key, 6), position), (shards_of,), jnp.float32, least / len(cuts), largest / len(cuts))
        factor_of = factor_of * jnp.repeat(jnp.exp(steps), extent[position] // shards_of).reshape((-1,) + (1,) * (len(extent) - 1 - position))
    return factor_of


def split_up(count, total, limit, slope):
    loads = [(1 << 20) // math.isqrt(standing ** slope) + 1 for standing in range(2, count + 1)]
    spare, counts = total - limit - (count - 1), [1] * (count - 1)
    while spare > 0:
        movable = [i for i in range(count - 1) if counts[i] < limit]
        whole, remaining = sum([loads[i] for i in movable]), spare
        for i in movable:
            addition = min(limit - counts[i], max(1, remaining * loads[i] // whole), spare)
            counts[i] = counts[i] + addition
            spare = spare - addition
    return np.array([limit] + counts)


def uneven_parts(rng, count, total, most, slope):
    if count == 2:
        one = jax.random.randint(rng, (), max(1, total - most), min(most, total - 1) + 1)
        return jnp.stack([one, total - one])
    lengths = jnp.asarray(split_up(count, total, most, slope), jnp.int32)
    couples = (count - 1) // 2
    giver, taker = lengths[1:1 + 2 * couples:2], lengths[2:2 + 2 * couples:2]
    slack = jnp.minimum(giver - 1, most - taker)
    shifted = jax.random.randint(jax.random.fold_in(rng, 1), (couples,), 0, 1 << 20) % (slack + 1)
    lengths = lengths.at[1:1 + 2 * couples:2].set(giver - shifted).at[2:2 + 2 * couples:2].set(taker + shifted)
    return lengths[jax.random.permutation(jax.random.fold_in(rng, 2), count)]


def noise(rng, shape, deviation, bound, cuts=(), kind=jnp.bfloat16):
    loudness = levels(rng, shape, cuts, -0.22, 0.18) if cuts else 1.0
    values = jax.random.normal(rng, shape, jnp.float32) * deviation * loudness
    return jnp.minimum(jnp.maximum(values, -bound), bound).astype(kind)


def heavy_noise(stream_key, shape, scale, limit, cuts, heavy, kind=jnp.bfloat16):
    drawn = scale * jax.random.normal(stream_key, shape, jnp.float32)
    if cuts:
        drawn = drawn * levels(stream_key, shape, cuts, -0.22, 0.18)
    return jnp.clip(strengthened(drawn, jax.random.fold_in(stream_key, 3), *heavy), -limit, limit).astype(kind)


def setup_inputs(seed: int = 0) -> dict:
    key_list = jax.random.split(jax.random.key(seed), 11)
    tokens = noise(key_list[0], (TOKENS, D), 1.0, 6.0, ((0, 64),))
    gain_one = jnp.clip(1.0 + 0.1 * jax.random.normal(key_list[1], (D,), jnp.float32), 0.5, 1.5)
    qkv_one = noise(key_list[2], (3, D, D), D ** -0.5, 0.1875, ((2, 4),))
    out_one = noise(key_list[3], (D, D), D ** -0.5, 0.1875, ((0, 4),))
    gain_two = jnp.clip(1.0 + 0.1 * jax.random.normal(key_list[4], (D,), jnp.float32), 0.5, 1.5)
    qkv_two = noise(key_list[5], (3, D, D), D ** -0.5, 0.1875, ((2, 4),))
    out_two = noise(key_list[6], (D, D), D ** -0.5, 0.1875, ((0, 4),))
    hilbert_pos = draw_hilbert_pos(jax.random.fold_in(key_list[10], 71), 0)
    scene = jnp.searchsorted(jnp.cumsum(uneven_parts(key_list[8], TOKENS * 4 // WINDOW, TOKENS, WINDOW // 2, 2)), jnp.arange(TOKENS), side="right").astype(jnp.int32)
    cotangent = heavy_noise(key_list[9], (TOKENS, D), 1.0, 16.0, ((0, 64),), (0, 1, 64, 4.0))
    return {"tokens": tokens, "gain_one": gain_one, "qkv_one": qkv_one, "out_one": out_one, "gain_two": gain_two, "qkv_two": qkv_two, "out_two": out_two, "hilbert_pos": hilbert_pos, "scene": scene, "cotangent": cotangent}


NORM_EPS = 1e-06

def normalize(layer_in, gain_vec):
    wide_in = layer_in.astype(jnp.float32)
    inv_rms = lax.rsqrt(lax.optimization_barrier(jnp.mean(wide_in * wide_in, axis=-1, keepdims=True)) + NORM_EPS)
    return ((wide_in * inv_rms * gain_vec).astype(jnp.bfloat16), inv_rms)

def project(normed, matrix):
    return jnp.dot(normed, matrix, preferred_element_type=jnp.float32).astype(jnp.bfloat16)

def split_heads(block):
    return block.reshape(block.shape[0], HEADS, HEAD_DIM).astype(jnp.float32)

def window_slice(array, window_idx):
    return lax.dynamic_slice_in_dim(array, window_idx * WINDOW, WINDOW, 0)

def attn_probs(queries, keys_win, scene_ids):
    scores = jnp.einsum('qhd,khd->hqk', queries, keys_win) * (1.0 / math.sqrt(HEAD_DIM))
    allowed = scene_ids[:, None] == scene_ids[None, :]
    weights_exp = jnp.where(allowed[None], jnp.exp(scores), 0.0)
    return weights_exp / lax.optimization_barrier(jnp.sum(weights_exp, axis=-1, keepdims=True))

def forward_attention(queries, keys_all, values_all, scene_ids):

    def one_window(window_idx):
        q_win = split_heads(window_slice(queries, window_idx))
        k_win = split_heads(window_slice(keys_all, window_idx))
        v_win = split_heads(window_slice(values_all, window_idx))
        probs_full = attn_probs(q_win, k_win, window_slice(scene_ids, window_idx))
        probs_low = lax.optimization_barrier(probs_full.astype(jnp.bfloat16)).astype(jnp.float32)
        mixed = jnp.einsum('hqk,khd->qhd', probs_low, v_win)
        return mixed.reshape(WINDOW, D).astype(jnp.bfloat16)
    count = queries.shape[0] // WINDOW
    return lax.map(one_window, jnp.arange(count, dtype=jnp.int32)).reshape(-1, D)

def backward_attention(queries, keys_all, values_all, scene_ids, d_out):

    def one_window(window_idx):
        q_win = split_heads(window_slice(queries, window_idx))
        k_win = split_heads(window_slice(keys_all, window_idx))
        v_win = split_heads(window_slice(values_all, window_idx))
        do_win = split_heads(window_slice(d_out, window_idx))
        probs_full = attn_probs(q_win, k_win, window_slice(scene_ids, window_idx))
        probs_low = lax.optimization_barrier(probs_full.astype(jnp.bfloat16)).astype(jnp.float32)
        d_probs = jnp.einsum('qhd,khd->hqk', do_win, v_win)
        d_values = jnp.einsum('hqk,qhd->khd', probs_low, do_win)
        d_scores = probs_full * (d_probs - lax.optimization_barrier(jnp.sum(d_probs * probs_full, axis=-1, keepdims=True)))
        d_low = d_scores * (1.0 / math.sqrt(HEAD_DIM))
        d_low = lax.optimization_barrier(d_low.astype(jnp.bfloat16)).astype(jnp.float32)
        d_queries = jnp.einsum('hqk,khd->qhd', d_low, k_win)
        d_keys = jnp.einsum('hqk,qhd->khd', d_low, q_win)
        return (d_queries.reshape(WINDOW, D).astype(jnp.bfloat16), d_keys.reshape(WINDOW, D).astype(jnp.bfloat16), d_values.reshape(WINDOW, D).astype(jnp.bfloat16))
    count = queries.shape[0] // WINDOW
    d_queries, d_keys, d_values = lax.map(one_window, jnp.arange(count, dtype=jnp.int32))
    return (d_queries.reshape(-1, D), d_keys.reshape(-1, D), d_values.reshape(-1, D))

def layer_forward(layer_in, gain_vec, qkv_mat, scene_ids):
    normed, inv_rms = normalize(layer_in, gain_vec)
    queries = project(normed, qkv_mat[0])
    keys_all = project(normed, qkv_mat[1])
    values_all = project(normed, qkv_mat[2])
    attn_out = forward_attention(queries, keys_all, values_all, scene_ids)
    return (normed, inv_rms, queries, keys_all, values_all, attn_out)

def layer_backward(layer_in, gain_vec, qkv_mat, out_mat, scene_ids, cot_in):
    normed, inv_rms, queries, keys_all, values_all, attn_out = layer_forward(layer_in, gain_vec, qkv_mat, scene_ids)
    grad_scale = 1.0 / math.sqrt(TOKENS)
    out_grad = jnp.dot(cot_in.T, attn_out, preferred_element_type=jnp.float32) * grad_scale
    d_out = jnp.dot(cot_in, out_mat.T, preferred_element_type=jnp.float32).astype(jnp.bfloat16)
    d_queries, d_keys, d_values = backward_attention(queries, keys_all, values_all, scene_ids, d_out)
    qkv_grad = jnp.stack([jnp.dot(normed.T, d_queries, preferred_element_type=jnp.float32), jnp.dot(normed.T, d_keys, preferred_element_type=jnp.float32), jnp.dot(normed.T, d_values, preferred_element_type=jnp.float32)]) * grad_scale
    d_normed = jnp.dot(d_queries, qkv_mat[0].T, preferred_element_type=jnp.float32)
    d_normed = d_normed + jnp.dot(d_keys, qkv_mat[1].T, preferred_element_type=jnp.float32)
    d_normed = d_normed + jnp.dot(d_values, qkv_mat[2].T, preferred_element_type=jnp.float32)
    wide_in = layer_in.astype(jnp.float32)
    gain_grad = lax.optimization_barrier(jnp.sum(d_normed * wide_in * inv_rms, axis=0)) * grad_scale
    d_scaled = d_normed * gain_vec
    d_input = cot_in.astype(jnp.float32) + inv_rms * (d_scaled - wide_in * inv_rms * inv_rms * lax.optimization_barrier(jnp.mean(d_scaled * wide_in, axis=-1, keepdims=True)))
    return (d_input.astype(jnp.bfloat16), qkv_grad, out_grad, gain_grad)

def reference(tokens, gain_one, qkv_one, out_one, gain_two, qkv_two, out_two, hilbert_pos, scene, cotangent):
    plain_ids = jnp.zeros((TOKENS,), jnp.int32)
    first = layer_forward(tokens, gain_one, qkv_one, plain_ids)
    mixed = jnp.dot(first[5], out_one, preferred_element_type=jnp.float32)
    first_out = (tokens.astype(jnp.float32) + mixed).astype(jnp.bfloat16)
    second_in = jnp.zeros_like(first_out).at[hilbert_pos].set(first_out)
    d_second, qkv_grad_two, out_grad_two, gain_grad_two = layer_backward(second_in, gain_two, qkv_two, out_two, scene, cotangent)
    d_first = d_second[hilbert_pos]
    grad_input, qkv_grad_one, out_grad_one, gain_grad_one = layer_backward(tokens, gain_one, qkv_one, out_one, plain_ids, d_first)
    return (grad_input, qkv_grad_one, out_grad_one, gain_grad_one, qkv_grad_two, out_grad_two, gain_grad_two)
```

```python
import jax
import jax.numpy as jnp
from jax import lax
from jax.experimental import pallas as pl
from jax.experimental.pallas import tpu as pltpu
from jax.sharding import PartitionSpec as P

MESH = pl.DeviceIdType.MESH
F32 = jnp.float32
BF16 = jnp.bfloat16
EPS = 1e-06
ROWS = 256
BLK = 256
NX = 4
NT = 64
NY = 4
NZ = 8
HEADS = 4
HD = 64
SLOTS = 8
GRAD_SCALE = 1.0 / 128.0

KV = 0
BACK = 2
RS = 4
ROWSUM = 16
AG = 24
A2A = 36
GC = 38
GY = 40
GZ = 48
NC = 64
NYS = 65
NZS = 69
NXS = 77
NSEM = 82


def dot(a, b):
    return lax.dot_general(a, b, (((1,), (0,)), ((), ())), preferred_element_type=F32)


def dot_nt(a, b):
    return lax.dot_general(a, b, (((1,), (1,)), ((), ())), preferred_element_type=F32)


def kernel(
    tokens, gain1, qkv1, out1, gain2, qkv2, out2, hpos, scene, cot,
    o_gin, o_qkv1, o_out1, o_qkv2, o_out2, o_gain,
    s_ref, st_ref, r_ref, rt_ref, bias_ref,
    h_ref, ht_ref, rinv_ref, kv_ref, kt_ref, vt_ref, q_ref, qt_ref, p_ref, pb_ref, obt_ref, ob_ref,
    do_ref, dot_ref, ds_ref, qstk_ref, dostk_ref, dqt_ref, dqkv_ref, kvs_ref, kvr_ref, ct_ref,
    rss_ref, rsr_ref, ms_ref, mr_ref, as_ref, ar_ref, ag_ref,
    g_ref, gc_ref, g2_ref, gy_ref, g3_ref, gz_ref,
    n0_ref, nc_ref, n1_ref, ny_ref, n2_ref, nz_ref, nx_ref,
    ssem, rsem,
):
    t = lax.axis_index("tok")
    x = lax.axis_index("head")
    core = lax.rem(t, 2)
    z = lax.rem(t // 2, NZ)
    y = t // (2 * NZ)
    mate = t + 1 - 2 * core
    gains, qkvs, outs = (gain1, gain2), (qkv1, qkv2), (out1, out2)

    def xdev(j):
        return {"head": lax.rem(x + j, NX)}

    def ydev(j):
        return {"tok": (lax.rem(y + j, NY) * NZ + z) * 2 + core}

    def zdev(j):
        return {"tok": (y * NZ + lax.rem(z + j, NZ)) * 2 + core}

    def remote(src, dst, sem, dev):
        return pltpu.make_async_remote_copy(
            src_ref=src, dst_ref=dst, send_sem=ssem.at[sem], recv_sem=rsem.at[sem],
            device_id=dev, device_id_type=MESH,
        )

    barrier = pltpu.get_barrier_semaphore()

    def greet(j, carry):
        pl.semaphore_signal(
            barrier, inc=1, device_id={"tok": lax.rem(t + j, NT)}, device_id_type=MESH
        )
        return carry

    lax.fori_loop(1, NT, greet, 0)
    for j in range(1, NX):
        pl.semaphore_signal(barrier, inc=1, device_id=xdev(j), device_id_type=MESH)

    sends = []

    def start(copy):
        copy.start()
        sends.append(copy)
        return copy

    def u_block(layer, b):
        if layer == 0:
            return tokens[:, b * BLK : (b + 1) * BLK].astype(F32)
        return ag_ref[0, b].astype(F32)

    def u_chunk(layer, at):
        if layer == 0:
            return tokens[:, pl.ds(pl.multiple_of(at * BLK, BLK), BLK)].astype(F32)
        return ag_ref[0, at].astype(F32)

    def cot_block(layer, b):
        return cot[:, b * BLK : (b + 1) * BLK] if layer == 1 else ag_ref[1, b]

    def cot_chunk(layer, at):
        if layer == 1:
            return cot[:, pl.ds(pl.multiple_of(at * BLK, BLK), BLK)]
        return ag_ref[1, at]

    def indices():
        lane_lt = lax.broadcasted_iota(jnp.int32, (ROWS, ROWS), 0) < lax.broadcasted_iota(
            jnp.int32, (ROWS, ROWS), 1
        )
        tri = jnp.where(lane_lt, 1.0, 0.0).astype(BF16)
        slot = lax.broadcasted_iota(jnp.int32, (NT * SLOTS, ROWS), 0).astype(F32)
        dev = lax.broadcasted_iota(jnp.int32, (NT, ROWS), 0)
        lane = lax.broadcasted_iota(jnp.int32, (NT, ROWS), 1).astype(F32)
        own = hpos[pl.ds(t, 1), :] // ROWS
        hit = jnp.where(dev == own, 1.0, 0.0)
        before = dot(hit.astype(BF16), tri)
        send_id = jnp.sum(hit * (before + dev.astype(F32) * SLOTS), axis=0, keepdims=True)
        s = jnp.where(slot == send_id, 1.0, 0.0)
        s_ref[...] = s.astype(BF16)
        st_ref[...] = s.T.astype(BF16)
        every = hpos[...]
        place = lax.rem(every, ROWS).astype(F32)
        mine = jnp.where(every // ROWS == t, 1.0, 0.0)
        rank = dot(mine.astype(BF16), tri)
        recv_id = jnp.zeros((1, ROWS), F32)
        for k in range(SLOTS):
            chosen = mine * jnp.where(rank == k, 1.0, 0.0)
            row = jnp.sum(chosen * (place + 1.0), axis=1, keepdims=True) - 1.0
            found = jnp.where(row == lane, dev.astype(F32) * SLOTS + k, 0.0)
            recv_id = recv_id + jnp.sum(found, axis=0, keepdims=True)
        r = jnp.where(slot == recv_id, 1.0, 0.0)
        rt_ref[...] = r.astype(BF16)
        r_ref[...] = r.T.astype(BF16)
        ids = scene[pl.ds(t, 1), :].astype(F32)
        for half, source in ((0, t), (1, mate)):
            row = scene[pl.ds(source, 1), :].astype(F32)
            col = jnp.broadcast_to(row, (128, ROWS)).T[:, :1]
            bias_ref[half] = jnp.where(col == ids, 0.0, -1e30)

    def normalize(layer):
        total = jnp.zeros((ROWS, 1), F32)
        for b in range(NX):
            ub = u_block(layer, b)
            total = total + jnp.sum(ub * ub, axis=1, keepdims=True)
        rinv = lax.rsqrt(total * (1.0 / (NX * BLK)) + EPS)
        rinv_ref[layer] = rinv
        for b in range(NX):
            hb = u_block(layer, b) * rinv * gains[layer][b : b + 1, :]
            h_ref[layer, :, b * BLK : (b + 1) * BLK] = hb.astype(BF16)

    def keys_values(layer):
        h = h_ref[layer]
        kv_ref[layer, 0, 0] = dot(h, qkvs[layer][1]).astype(BF16)
        kv_ref[layer, 0, 1] = dot(h, qkvs[layer][2]).astype(BF16)

    def send_kv(layer):
        return start(
            remote(kv_ref.at[layer, 0], kv_ref.at[layer, 1], KV + layer, {"tok": mate})
        )

    row_head = lax.broadcasted_iota(jnp.int32, (BLK, ROWS), 0) // HD
    lane_head = lax.broadcasted_iota(jnp.int32, (ROWS, BLK), 1) // HD

    def queries(layer):
        q = dot(h_ref[layer], qkvs[layer][0]).astype(BF16).astype(F32) * 0.125
        q_ref[layer] = q.astype(BF16)
        qt = q.T
        for n in range(HEADS):
            qt_ref[:, n * ROWS : (n + 1) * ROWS] = jnp.where(row_head == n, qt, 0.0).astype(BF16)

    def attend(layer):
        for half in range(2):
            kt_ref[layer, half] = kv_ref[layer, half, 0].T
            vt_ref[layer, half] = kv_ref[layer, half, 1].T
        for n in range(HEADS):
            cols = slice(n * ROWS, (n + 1) * ROWS)
            rows = slice(n * HD, (n + 1) * HD)
            e = []
            for half in range(2):
                scores = dot(kv_ref[layer, half, 0], qt_ref[:, cols])
                if layer == 1:
                    scores = scores + bias_ref[half]
                e.append(jnp.exp(scores))
            total = jnp.sum(e[0], axis=0, keepdims=True) + jnp.sum(e[1], axis=0, keepdims=True)
            inv = 1.0 / total
            mixed = jnp.zeros((HD, ROWS), F32)
            for half in range(2):
                p = e[half] * inv
                p_ref[layer, half, :, cols] = p
                pb = p.astype(BF16)
                pb_ref[layer, half, :, cols] = pb
                mixed = mixed + dot(vt_ref[layer, half, rows, :], pb)
            obt_ref[rows, :] = mixed.astype(BF16)
        ob_ref[layer] = obt_ref[...].T

    def turn_h(layer):
        for b in range(NX):
            ht_ref[layer, b * BLK : (b + 1) * BLK, :] = h_ref[layer, :, b * BLK : (b + 1) * BLK].T

    def pull_back_out(layer):
        acc = jnp.zeros((ROWS, BLK), F32)
        for b in range(NX):
            acc = acc + dot_nt(cot_block(layer, b), outs[layer][:, b * BLK : (b + 1) * BLK])
        do = acc.astype(BF16)
        do_ref[...] = do
        dot_ref[...] = do.T
        for n in range(HEADS):
            dostk_ref[n * ROWS : (n + 1) * ROWS, :] = jnp.where(
                lane_head == n, do.astype(F32), 0.0
            ).astype(BF16)

    def attend_back(layer):
        q = q_ref[layer].astype(F32)
        dt = dot_ref[...].astype(F32)
        for n in range(HEADS):
            cols = slice(n * ROWS, (n + 1) * ROWS)
            rows = slice(n * HD, (n + 1) * HD)
            qstk_ref[n * ROWS : (n + 1) * ROWS, :] = jnp.where(lane_head == n, q, 0.0).astype(BF16)
            only = jnp.where(row_head == n, dt, 0.0).astype(BF16)
            dp = [dot(kv_ref[layer, half, 1], only) for half in range(2)]
            p = [p_ref[layer, half, :, cols] for half in range(2)]
            r = jnp.sum(dp[0] * p[0], axis=0, keepdims=True) + jnp.sum(
                dp[1] * p[1], axis=0, keepdims=True
            )
            dq = jnp.zeros((HD, ROWS), F32)
            for half in range(2):
                ds = (p[half] * (dp[half] - r)).astype(BF16)
                ds_ref[half, :, cols] = ds
                dq = dq + dot(kt_ref[layer, half, rows, :], ds)
            dqt_ref[rows, :] = (dq * 0.125).astype(BF16)
        kvs_ref[layer, 0] = dot(ds_ref[1], qstk_ref[...]).astype(BF16)
        kvs_ref[layer, 1] = dot(pb_ref[layer, 1], dostk_ref[...]).astype(BF16)
        copy = start(
            remote(kvs_ref.at[layer], kvr_ref.at[layer], BACK + layer, {"tok": mate})
        )
        dqkv_ref[0] = dqt_ref[...].T
        dk = dot(ds_ref[0], qstk_ref[...])
        dv = dot(pb_ref[layer, 0], dostk_ref[...])
        copy.wait_recv()
        dqkv_ref[1] = (dk + kvr_ref[layer, 0].astype(F32)).astype(BF16)
        dqkv_ref[2] = (dv + kvr_ref[layer, 1].astype(F32)).astype(BF16)

    def dh_part(layer, at):
        rows = pl.ds(pl.multiple_of(at * BLK, BLK), BLK)
        acc = dot_nt(dqkv_ref[0], qkvs[layer][0, rows, :])
        acc = acc + dot_nt(dqkv_ref[1], qkvs[layer][1, rows, :])
        return acc + dot_nt(dqkv_ref[2], qkvs[layer][2, rows, :])

    def send_dh(layer):
        phase = 2 - layer
        sums = jnp.zeros((ROWS, 1), F32)
        copies = []
        own = None
        for j in (2, 1, 3, 0):
            at = lax.rem(x + j, NX)
            part = dh_part(layer, at)
            weight = u_chunk(layer, at) * gains[layer][pl.ds(at, 1), :]
            sums = sums + jnp.sum(part * weight, axis=1, keepdims=True)
            if j:
                rss_ref[phase, j] = part.astype(BF16)
                copies.append(
                    start(
                        remote(
                            rss_ref.at[phase, j], rsr_ref.at[phase, j], RS + 4 * phase + j, xdev(j)
                        )
                    )
                )
            else:
                own = part
        ms_ref[layer] = jnp.broadcast_to(sums, (ROWS, 128)).T[:8, :]
        for j in (2, 1, 3):
            copies.append(
                start(
                    remote(
                        ms_ref.at[layer], mr_ref.at[layer, j], ROWSUM + 4 * layer + j, xdev(j)
                    )
                )
            )
        rss_ref_own[layer] = own
        return copies

    rss_ref_own = {}

    def finish_dh(layer, copies):
        phase = 2 - layer
        for copy in copies:
            copy.wait_recv()
        dh = rss_ref_own[layer]
        sums = ms_ref[layer]
        for j in range(1, NX):
            dh = dh + rsr_ref[phase, j].astype(F32)
            sums = sums + mr_ref[layer, j]
        mean = jnp.broadcast_to(sums[:1, :], (128, ROWS)).T[:, :1] * (1.0 / (NX * BLK))
        u = u_chunk(layer, x)
        rinv = rinv_ref[layer]
        n0_ref[layer : layer + 1, :] = jnp.sum(dh * u * rinv, axis=0, keepdims=True)
        scaled = dh * gains[layer][pl.ds(x, 1), :]
        du = cot_chunk(layer, x).astype(F32) + rinv * (scaled - u * rinv * rinv * mean)
        return du.astype(BF16)

    def relay_out(way, table, chunk):
        a = dot(table[...], chunk)
        lo = a[:, :128].reshape(NT, SLOTS, 128)
        hi = a[:, 128:].reshape(NT, SLOTS, 128)
        as_ref[way] = jnp.concatenate([lo, hi], axis=1).astype(BF16)
        ar_ref[way, t] = as_ref[way, t]

        def push(j, carry):
            to = lax.rem(t + j, NT)
            remote(as_ref.at[way, to], ar_ref.at[way, t], A2A + way, {"tok": to}).start()
            return carry

        lax.fori_loop(1, NT, push, 0)
        every = pl.ds(0, NT - 1)
        copy = remote(as_ref.at[way, every], ar_ref.at[way, every], A2A + way, {"tok": mate})
        sends.append(copy)
        return copy

    def relay_in(way, table, copy):
        copy.wait_recv()
        a = ar_ref[way].astype(F32)
        lo = a[:, :SLOTS, :].reshape(NT * SLOTS, 128)
        hi = a[:, SLOTS:, :].reshape(NT * SLOTS, 128)
        return dot(table[...], jnp.concatenate([lo, hi], axis=1).astype(BF16)).astype(BF16)

    def spread(phase, chunk):
        ag_ref[phase, x] = chunk
        copies = []
        for j in (2, 1, 3):
            copies.append(
                start(
                    remote(ag_ref.at[phase, x], ag_ref.at[phase, x], AG + 4 * phase + j, xdev(j))
                )
            )
        return copies

    def turn_cot(layer):
        for b in range(NX):
            ct_ref[b * BLK : (b + 1) * BLK, :] = cot_block(layer, b).T

    def put_grad(layer, kind, b, value):
        parts = value.reshape(NZ, 2, 16, BLK)
        for c in range(2):
            g_ref[layer, c, b * NZ : (b + 1) * NZ, kind * 16 : (kind + 1) * 16, :] = parts[
                :, c
            ].astype(BF16)

    def out_grads(layer):
        for b in range(NX):
            put_grad(layer, 3, b, dot(ct_ref[b * BLK : (b + 1) * BLK, :], ob_ref[layer]))

    def qkv_grads(layer):
        for b in range(NX):
            left = ht_ref[layer, b * BLK : (b + 1) * BLK, :]
            for kind in range(3):
                put_grad(layer, kind, b, dot(left, dqkv_ref[kind]))

    def grads_core(layer):
        return start(
            remote(g_ref.at[layer, 1 - core], gc_ref.at[layer], GC + layer, {"tok": mate})
        )

    def grads_y(layer, copy):
        copy.wait_recv()
        copies = []
        for j in (2, 1, 3, 0):
            rows = pl.ds(lax.rem(y + j, NY) * NZ, NZ)
            value = g_ref[layer, core, rows].astype(F32) + gc_ref[layer, rows].astype(F32)
            g2_ref[layer, j] = value.astype(BF16)
            if j:
                copies.append(
                    start(
                        remote(g2_ref.at[layer, j], gy_ref.at[layer, j], GY + 4 * layer + j, ydev(j))
                    )
                )
        return copies

    def grads_z(layer, copies):
        for copy in copies:
            copy.wait_recv()
        later = []
        for j in (4, 3, 5, 2, 6, 1, 7, 0):
            at = lax.rem(z + j, NZ)
            value = g2_ref[layer, 0, at].astype(F32)
            for k in range(1, NY):
                value = value + gy_ref[layer, k, at].astype(F32)
            g3_ref[layer, j] = value.astype(BF16)
            if j:
                later.append(
                    start(
                        remote(g3_ref.at[layer, j], gz_ref.at[layer, j], GZ + 8 * layer + j, zdev(j))
                    )
                )
        return later

    def grads_end(layer, copies):
        for copy in copies:
            copy.wait_recv()
        value = g3_ref[layer, 0].astype(F32)
        for j in range(1, NZ):
            value = value + gz_ref[layer, j].astype(F32)
        value = value * GRAD_SCALE
        o_qkv, o_out = ((o_qkv1, o_out1), (o_qkv2, o_out2))[layer]
        for kind in range(3):
            o_qkv[kind] = value[kind * 16 : (kind + 1) * 16, :]
        o_out[...] = value[48:64, :]

    normalize(0)
    keys_values(0)
    pl.semaphore_wait(barrier, NT - 1 + NX - 1)
    kv_copy = send_kv(0)
    queries(0)
    turn_h(0)
    indices()
    n0_ref[...] = jnp.zeros_like(n0_ref)
    kv_copy.wait_recv()
    attend(0)
    copies = []
    own = None
    for j in (2, 1, 3, 0):
        at = pl.multiple_of(lax.rem(x + j, NX) * BLK, BLK)
        part = dot(ob_ref[0], out1[:, pl.ds(at, BLK)])
        if j:
            rss_ref[0, j] = part.astype(BF16)
            copies.append(start(remote(rss_ref.at[0, j], rsr_ref.at[0, j], RS + j, xdev(j))))
        else:
            own = part
    y1 = own
    for copy in copies:
        copy.wait_recv()
    for j in range(1, NX):
        y1 = y1 + rsr_ref[0, j].astype(F32)
    y1 = (u_chunk(0, x) + y1).astype(BF16)
    relay = relay_out(0, s_ref, y1)
    pull_back_out(1)
    turn_cot(1)
    copies = spread(0, relay_in(0, r_ref, relay))
    for copy in copies:
        copy.wait_recv()

    normalize(1)
    keys_values(1)
    kv_copy = send_kv(1)
    queries(1)
    turn_h(1)
    kv_copy.wait_recv()
    attend(1)
    attend_back(1)
    copies = send_dh(1)
    out_grads(1)
    qkv_grads(1)
    core_copy = grads_core(1)
    du2 = finish_dh(1, copies)
    relay = relay_out(1, rt_ref, du2)
    y_copies = grads_y(1, core_copy)
    copies = spread(1, relay_in(1, st_ref, relay))
    z_copies = grads_z(1, y_copies)
    for copy in copies:
        copy.wait_recv()

    pull_back_out(0)
    attend_back(0)
    copies = send_dh(0)
    grads_end(1, z_copies)
    turn_cot(0)
    out_grads(0)
    qkv_grads(0)
    core_copy = grads_core(0)
    du1 = finish_dh(0, copies)
    copies = spread(2, du1)
    gain_copy = start(remote(n0_ref, nc_ref, NC, {"tok": mate}))
    y_copies = grads_y(0, core_copy)
    gain_copy.wait_recv()
    n1_ref[...] = n0_ref[...] + nc_ref[...]
    gain_copies = [start(remote(n1_ref, ny_ref.at[j], NYS + j, ydev(j))) for j in range(1, NY)]
    for copy in copies:
        copy.wait_recv()
    for b in range(NX):
        o_gin[:, b * BLK : (b + 1) * BLK] = ag_ref[2, b]
    for copy in gain_copies:
        copy.wait_recv()
    n2_ref[...] = n1_ref[...] + ny_ref[1] + ny_ref[2] + ny_ref[3]
    gain_copies = [start(remote(n2_ref, nz_ref.at[j], NZS + j, zdev(j))) for j in range(1, NZ)]
    z_copies = grads_z(0, y_copies)
    for copy in gain_copies:
        copy.wait_recv()
    value = n2_ref[...]
    for j in range(1, NZ):
        value = value + nz_ref[j]
    nx_ref[x] = value * GRAD_SCALE
    gain_copies = [start(remote(nx_ref.at[x], nx_ref.at[x], NXS + j, xdev(j))) for j in range(1, NX)]
    grads_end(0, z_copies)
    for copy in gain_copies:
        copy.wait_recv()
    o_gain[...] = nx_ref[t // (NT // NX)]
    for copy in sends:
        copy.wait_send()


def scratch():
    def b16(*shape):
        return pltpu.VMEM(shape, BF16)

    def f32(*shape):
        return pltpu.VMEM(shape, F32)

    wide = NT * SLOTS
    return [
        b16(wide, ROWS), b16(ROWS, wide), b16(ROWS, wide), b16(wide, ROWS), f32(2, ROWS, ROWS),
        b16(2, ROWS, NX * BLK), b16(2, NX * BLK, ROWS), f32(2, ROWS, 1),
        b16(2, 2, 2, ROWS, BLK), b16(2, 2, BLK, ROWS), b16(2, 2, BLK, ROWS),
        b16(2, ROWS, BLK), b16(BLK, HEADS * ROWS), f32(2, 2, ROWS, HEADS * ROWS),
        b16(2, 2, ROWS, HEADS * ROWS), b16(BLK, ROWS), b16(2, ROWS, BLK),
        b16(ROWS, BLK), b16(BLK, ROWS), b16(2, ROWS, HEADS * ROWS), b16(HEADS * ROWS, BLK),
        b16(HEADS * ROWS, BLK), b16(BLK, ROWS), b16(3, ROWS, BLK), b16(2, 2, ROWS, BLK),
        b16(2, 2, ROWS, BLK), b16(NX * BLK, ROWS),
        b16(3, NX, ROWS, BLK), b16(3, NX, ROWS, BLK), f32(2, 8, ROWS), f32(2, NX, 8, ROWS),
        b16(2, NT, 2 * SLOTS, 128), b16(2, NT, 2 * SLOTS, 128), b16(3, NX, ROWS, BLK),
        b16(2, 2, NY * NZ, 64, BLK), b16(2, NY * NZ, 64, BLK), b16(2, NY, NZ, 64, BLK),
        b16(2, NY, NZ, 64, BLK), b16(2, NZ, 64, BLK), b16(2, NZ, 64, BLK),
        f32(8, BLK), f32(8, BLK), f32(8, BLK), f32(NY, 8, BLK), f32(8, BLK), f32(NZ, 8, BLK),
        f32(NX, 8, BLK),
        pltpu.SemaphoreType.DMA((NSEM,)), pltpu.SemaphoreType.DMA((NSEM,)),
    ]


def local(
    tokens, gain_one, qkv_one, out_one, gain_two, qkv_two, out_two, hilbert_pos, scene, cotangent
):
    vmem = pl.BlockSpec(memory_space=pltpu.VMEM)
    grads = [
        jax.ShapeDtypeStruct((3, 16, BLK), F32),
        jax.ShapeDtypeStruct((16, BLK), F32),
    ]
    grad_input, qkv1, out1, qkv2, out2, gains = pl.pallas_call(
        kernel,
        out_shape=[
            jax.ShapeDtypeStruct((ROWS, NX * BLK), BF16),
            *grads,
            *grads,
            jax.ShapeDtypeStruct((8, BLK), F32),
        ],
        in_specs=[vmem] * 10,
        out_specs=[vmem] * 6,
        scratch_shapes=scratch(),
        compiler_params=pltpu.CompilerParams(
            collective_id=0, has_side_effects=True, vmem_limit_bytes=58 * 2**20
        ),
    )(
        tokens,
        gain_one.reshape(NX, BLK),
        qkv_one,
        out_one,
        gain_two.reshape(NX, BLK),
        qkv_two,
        out_two,
        hilbert_pos.reshape(NT, ROWS),
        scene.reshape(NT, ROWS),
        cotangent,
    )
    at = lax.rem(lax.axis_index("tok"), NT // NX) * 16
    mine = lax.dynamic_slice(gains, (0, at), (2, 16))
    return grad_input, qkv1, out1, mine[0], qkv2, out2, mine[1]


def solution(mesh):
    in_specs = (
        P("tok", None),
        P(),
        P(None, None, "head"),
        P("head", None),
        P(),
        P(None, None, "head"),
        P("head", None),
        P(),
        P(),
        P("tok", None),
    )
    out_specs = (
        P("tok", None),
        P(None, "tok", "head"),
        P("tok", "head"),
        P("tok"),
        P(None, "tok", "head"),
        P("tok", "head"),
        P("tok"),
    )
    return jax.shard_map(local, mesh=mesh, in_specs=in_specs, out_specs=out_specs, check_vma=False)
```

```python
import jax
import jax.numpy as jnp
from jax import lax
from jax.experimental import pallas as pl
from jax.experimental.pallas import tpu as pltpu
from jax.sharding import PartitionSpec as P

MESH = pl.DeviceIdType.MESH
F32 = jnp.float32
BF16 = jnp.bfloat16
EPS = 1e-06
ROWS = 256
BLK = 256
NX = 4
NT = 64
NY = 4
NZ = 8
HEADS = 4
HD = 64
SLOTS = 8
GRAD_SCALE = 1.0 / 128.0

HALF = 128

KV = 0
BACK = 2
A2A = 4
GC = 8
ROWSUM = 12
NC = 20
NYS = 20
NXS = 24
NZS = 28
RS = 36
AG = 60
GY = 84
GZ = 100
NSEM = 132


def dot(a, b):
    return lax.dot_general(a, b, (((1,), (0,)), ((), ())), preferred_element_type=F32)


def dot_nt(a, b):
    return lax.dot_general(a, b, (((1,), (1,)), ((), ())), preferred_element_type=F32)


def kernel(
    tokens_in, gain1, qkv1_in, out1_in, gain2, qkv2_in, out2_in, hpos, scene, cot_in,
    o_gin, o_qkv1, o_out1, o_qkv2, o_out2, o_gain,
    tokens, qkv1, out1, qkv2, out2, cot,
    s_ref, st_ref, r_ref, rt_ref, bias_ref,
    h_ref, ht_ref, rinv_ref, kv_ref, kt_ref, vt_ref, q_ref, qt_ref, p_ref, pb_ref, obt_ref, ob_ref,
    do_ref, dot_ref, ds_ref, qstk_ref, dostk_ref, dqt_ref, dqkv_ref, kvs_ref, kvr_ref, ct_ref,
    rss_ref, rsr_ref, ms_ref, mr_ref, as_ref, ar_ref, ag_ref,
    g_ref, gc_ref, g2_ref, gy_ref, g3_ref, gz_ref,
    n0_ref, nc_ref, n1_ref, ny_ref, n2_ref, nz_ref, n3_ref, nx_ref,
    ssem, rsem, lsem, y_known, all_known,
):
    t = lax.axis_index("tok")
    x = lax.axis_index("head")
    core = lax.rem(t, 2)
    z = lax.rem(t // 2, NZ)
    y = t // (2 * NZ)
    mate = t + 1 - 2 * core
    gains, qkvs, outs = (gain1, gain2), (qkv1, qkv2), (out1, out2)

    def xdev(j):
        return {"head": lax.rem(x + j, NX)}

    def ydev(j):
        return {"tok": (lax.rem(y + j, NY) * NZ + z) * 2 + core}

    def zdev(j):
        return {"tok": (y * NZ + lax.rem(z + j, NZ)) * 2 + core}

    def remote(src, dst, sem, dev):
        return pltpu.make_async_remote_copy(
            src_ref=src, dst_ref=dst, send_sem=ssem.at[sem], recv_sem=rsem.at[sem],
            device_id=dev, device_id_type=MESH,
        )

    loads = [
        pltpu.make_async_copy(source, target, lsem.at[i])
        for i, (source, target) in enumerate(
            (
                (tokens_in, tokens),
                (qkv1_in, qkv1),
                (out1_in, out1),
                (qkv2_in, qkv2),
                (out2_in, out2),
                (cot_in, cot),
            )
        )
    ]
    for load in loads:
        load.start()
    barrier = pltpu.get_barrier_semaphore()

    near = [{"tok": mate}]
    near += [xdev(j) for j in range(1, NX)]
    near += [ydev(j) for j in range(1, NY)]
    near += [zdev(j) for j in range(1, NZ)]
    for dev in near:
        pl.semaphore_signal(barrier, inc=1, device_id=dev, device_id_type=MESH)

    sends = []

    def start(copy):
        copy.start()
        sends.append(copy)
        return copy

    def gathered(phase, b):
        return jnp.concatenate([ag_ref[phase, 0, b], ag_ref[phase, 1, b]], axis=1)

    def u_block(layer, b):
        if layer == 0:
            return tokens[:, b * BLK : (b + 1) * BLK].astype(F32)
        return gathered(0, b).astype(F32)

    def half_cols(at, half):
        return pl.ds(pl.multiple_of(at * BLK + half * HALF, HALF), HALF)

    def u_part(layer, at, half):
        if layer == 0:
            return tokens[:, half_cols(at, half)].astype(F32)
        return ag_ref[0, half, at].astype(F32)

    def gain_part(layer, at, half):
        return gains[layer][pl.ds(2 * at + half, 1), :]

    def cot_block(layer, b):
        return cot[:, b * BLK : (b + 1) * BLK] if layer == 1 else gathered(1, b)

    def cot_part(layer, half):
        if layer == 1:
            return cot[:, half_cols(x, half)].astype(F32)
        return ag_ref[1, half, x].astype(F32)

    def wide_row(ref, at):
        return jnp.concatenate([ref[pl.ds(2 * at, 1), :], ref[pl.ds(2 * at + 1, 1), :]], axis=1)

    def indices():
        lane_lt = lax.broadcasted_iota(jnp.int32, (ROWS, ROWS), 0) < lax.broadcasted_iota(
            jnp.int32, (ROWS, ROWS), 1
        )
        tri = jnp.where(lane_lt, 1.0, 0.0).astype(BF16)
        slot = lax.broadcasted_iota(jnp.int32, (NT * SLOTS, ROWS), 0).astype(F32)
        dev = lax.broadcasted_iota(jnp.int32, (NT, ROWS), 0)
        lane = lax.broadcasted_iota(jnp.int32, (NT, ROWS), 1).astype(F32)
        own = wide_row(hpos, t) // ROWS
        hit = jnp.where(dev == own, 1.0, 0.0)
        before = dot(hit.astype(BF16), tri)
        send_id = jnp.sum(hit * (before + dev.astype(F32) * SLOTS), axis=0, keepdims=True)
        s = jnp.where(slot == send_id, 1.0, 0.0)
        s_ref[...] = s.astype(BF16)
        st_ref[...] = s.T.astype(BF16)
        every = jnp.concatenate([hpos[0::2, :], hpos[1::2, :]], axis=1)
        place = lax.rem(every, ROWS).astype(F32)
        mine = jnp.where(every // ROWS == t, 1.0, 0.0)
        rank = dot(mine.astype(BF16), tri)
        recv_id = jnp.zeros((1, ROWS), F32)
        for k in range(SLOTS):
            chosen = mine * jnp.where(rank == k, 1.0, 0.0)
            row = jnp.sum(chosen * (place + 1.0), axis=1, keepdims=True) - 1.0
            found = jnp.where(row == lane, dev.astype(F32) * SLOTS + k, 0.0)
            recv_id = recv_id + jnp.sum(found, axis=0, keepdims=True)
        r = jnp.where(slot == recv_id, 1.0, 0.0)
        rt_ref[...] = r.astype(BF16)
        r_ref[...] = r.T.astype(BF16)
        ids = wide_row(scene, t).astype(F32)
        for half, source in ((0, t), (1, mate)):
            row = wide_row(scene, source).astype(F32)
            col = jnp.broadcast_to(row, (128, ROWS)).T[:, :1]
            bias_ref[half] = jnp.where(col == ids, 0.0, -1e30)

    def normalize(layer):
        total = jnp.zeros((ROWS, 1), F32)
        for b in range(NX):
            ub = u_block(layer, b)
            total = total + jnp.sum(ub * ub, axis=1, keepdims=True)
        rinv = lax.rsqrt(total * (1.0 / (NX * BLK)) + EPS)
        rinv_ref[layer] = rinv
        for b in range(NX):
            hb = u_block(layer, b) * rinv * wide_row(gains[layer], b)
            h_ref[layer, :, b * BLK : (b + 1) * BLK] = hb.astype(BF16)

    def keys_values(layer):
        h = h_ref[layer]
        kv_ref[layer, 0, 0] = dot(h, qkvs[layer][1]).astype(BF16)
        kv_ref[layer, 0, 1] = dot(h, qkvs[layer][2]).astype(BF16)

    def send_kv(layer):
        return start(
            remote(kv_ref.at[layer, 0], kv_ref.at[layer, 1], KV + layer, {"tok": mate})
        )

    row_head = lax.broadcasted_iota(jnp.int32, (BLK, ROWS), 0) // HD
    lane_head = lax.broadcasted_iota(jnp.int32, (ROWS, BLK), 1) // HD

    def queries(layer):
        q = dot(h_ref[layer], qkvs[layer][0]).astype(BF16).astype(F32) * 0.125
        q_ref[layer] = q.astype(BF16)
        qt = q.T
        for n in range(HEADS):
            qt_ref[:, n * ROWS : (n + 1) * ROWS] = jnp.where(row_head == n, qt, 0.0).astype(BF16)

    def attend(layer):
        for half in range(2):
            kt_ref[layer, half] = kv_ref[layer, half, 0].T
            vt_ref[layer, half] = kv_ref[layer, half, 1].T
        for n in range(HEADS):
            cols = slice(n * ROWS, (n + 1) * ROWS)
            rows = slice(n * HD, (n + 1) * HD)
            e = []
            for half in range(2):
                scores = dot(kv_ref[layer, half, 0], qt_ref[:, cols])
                if layer == 1:
                    scores = scores + bias_ref[half]
                e.append(jnp.exp(scores))
            total = jnp.sum(e[0], axis=0, keepdims=True) + jnp.sum(e[1], axis=0, keepdims=True)
            inv = 1.0 / total
            mixed = jnp.zeros((HD, ROWS), F32)
            for half in range(2):
                p = e[half] * inv
                p_ref[layer, half, :, cols] = p
                pb = p.astype(BF16)
                pb_ref[layer, half, :, cols] = pb
                mixed = mixed + dot(vt_ref[layer, half, rows, :], pb)
            obt_ref[rows, :] = mixed.astype(BF16)
        ob_ref[layer] = obt_ref[...].T

    def turn_h(layer):
        for b in range(NX):
            ht_ref[layer, b * BLK : (b + 1) * BLK, :] = h_ref[layer, :, b * BLK : (b + 1) * BLK].T

    def pull_back_out(layer):
        acc = jnp.zeros((ROWS, BLK), F32)
        for b in range(NX):
            acc = acc + dot_nt(cot_block(layer, b), outs[layer][:, b * BLK : (b + 1) * BLK])
        do = acc.astype(BF16)
        do_ref[...] = do
        dot_ref[...] = do.T
        for n in range(HEADS):
            dostk_ref[n * ROWS : (n + 1) * ROWS, :] = jnp.where(
                lane_head == n, do.astype(F32), 0.0
            ).astype(BF16)

    def attend_back(layer, early, core_copies):
        q = q_ref[layer].astype(F32)
        dt = dot_ref[...].astype(F32)
        for n in range(HEADS):
            cols = slice(n * ROWS, (n + 1) * ROWS)
            rows = slice(n * HD, (n + 1) * HD)
            qstk_ref[n * ROWS : (n + 1) * ROWS, :] = jnp.where(lane_head == n, q, 0.0).astype(BF16)
            only = jnp.where(row_head == n, dt, 0.0).astype(BF16)
            dp = [dot(kv_ref[layer, half, 1], only) for half in range(2)]
            p = [p_ref[layer, half, :, cols] for half in range(2)]
            r = jnp.sum(dp[0] * p[0], axis=0, keepdims=True) + jnp.sum(
                dp[1] * p[1], axis=0, keepdims=True
            )
            dq = jnp.zeros((HD, ROWS), F32)
            for half in range(2):
                ds = (p[half] * (dp[half] - r)).astype(BF16)
                ds_ref[half, :, cols] = ds
                dq = dq + dot(kt_ref[layer, half, rows, :], ds)
            dqt_ref[rows, :] = (dq * 0.125).astype(BF16)
        kvs_ref[layer, 0] = dot(ds_ref[1], qstk_ref[...]).astype(BF16)
        kvs_ref[layer, 1] = dot(pb_ref[layer, 1], dostk_ref[...]).astype(BF16)
        copy = start(
            remote(kvs_ref.at[layer], kvr_ref.at[layer], BACK + layer, {"tok": mate})
        )
        dqkv_ref[0] = dqt_ref[...].T
        dk = dot(ds_ref[0], qstk_ref[...])
        dv = dot(pb_ref[layer, 0], dostk_ref[...])
        if early:
            turn_cot(layer)
            early_grads(layer)
            core_copies.append(grads_core(layer, 0))
        copy.wait_recv()
        dqkv_ref[1] = (dk + kvr_ref[layer, 0].astype(F32)).astype(BF16)
        dqkv_ref[2] = (dv + kvr_ref[layer, 1].astype(F32)).astype(BF16)

    def dh_part(layer, at, half):
        rows = half_cols(at, half)
        acc = dot_nt(dqkv_ref[0], qkvs[layer][0, rows, :])
        acc = acc + dot_nt(dqkv_ref[1], qkvs[layer][1, rows, :])
        return acc + dot_nt(dqkv_ref[2], qkvs[layer][2, rows, :])

    def send_part(phase, half, j, part):
        rss_ref[phase, half, j] = part.astype(BF16)
        sem = RS + 8 * phase + 4 * half + j
        return start(remote(rss_ref.at[phase, half, j], rsr_ref.at[phase, half, j], sem, xdev(j)))

    def send_dh(layer):
        phase = 2 - layer
        sums = jnp.zeros((ROWS, 1), F32)
        copies = ([], [])
        own = [None, None]
        rinv = rinv_ref[layer]
        for half in range(2):
            for j in (2, 1, 3, 0):
                at = lax.rem(x + j, NX)
                part = dh_part(layer, at, half)
                if j:
                    copies[half].append(send_part(phase, half, j, part))
                else:
                    own[half] = part
                weighted = part * u_part(layer, at, half)
                sums = sums + jnp.sum(
                    weighted * gain_part(layer, at, half), axis=1, keepdims=True
                )
                n0_ref[at, layer : layer + 1, half * HALF : (half + 1) * HALF] = jnp.sum(
                    weighted * rinv, axis=0, keepdims=True
                )
        ms_ref[layer] = jnp.broadcast_to(sums, (ROWS, 128)).T[:8, :]
        for j in (2, 1, 3):
            sem = ROWSUM + 4 * layer + j
            copies[0].append(start(remote(ms_ref.at[layer], mr_ref.at[layer, j], sem, xdev(j))))
        return own, copies

    def row_mean(layer):
        sums = ms_ref[layer]
        for j in range(1, NX):
            sums = sums + mr_ref[layer, j]
        return jnp.broadcast_to(sums[:1, :], (128, ROWS)).T[:, :1] * (1.0 / (NX * BLK))

    def wait_all(copies):
        for copy in copies:
            copy.wait_recv()

    def total_part(phase, half, own):
        for j in range(1, NX):
            own = own + rsr_ref[phase, half, j].astype(F32)
        return own

    def finish_dh(layer, half, dh, mean):
        u = u_part(layer, x, half)
        rinv = rinv_ref[layer]
        scaled = dh * gain_part(layer, x, half)
        du = cot_part(layer, half) + rinv * (scaled - u * rinv * rinv * mean)
        return du.astype(BF16)

    def relay_out(way, half, table, chunk):
        packed = dot(table[...], chunk).reshape(NT, SLOTS, HALF)
        as_ref[way, half] = packed.astype(BF16)
        ar_ref[way, half, t] = as_ref[way, half, t]
        sem = A2A + 2 * way + half

        def push(j, carry):
            to = lax.rem(t + j, NT)
            remote(as_ref.at[way, half, to], ar_ref.at[way, half, t], sem, {"tok": to}).start()
            return carry

        lax.fori_loop(1, NT, push, 0)
        every = pl.ds(0, NT - 1)
        copy = remote(
            as_ref.at[way, half, every], ar_ref.at[way, half, every], sem, {"tok": mate}
        )
        sends.append(copy)
        return copy

    def relay_in(way, half, table, copy):
        copy.wait_recv()
        packed = ar_ref[way, half].astype(F32).reshape(NT * SLOTS, HALF).astype(BF16)
        return dot(table[...], packed).astype(BF16)

    def spread(phase, half, chunk):
        ag_ref[phase, half, x] = chunk
        place = ag_ref.at[phase, half, x]
        sem = AG + 8 * phase + 4 * half
        return [start(remote(place, place, sem + j, xdev(j))) for j in (2, 1, 3)]

    def turn_cot(layer):
        for b in range(NX):
            ct_ref[b * BLK : (b + 1) * BLK, :] = cot_block(layer, b).T

    def put_grad(layer, part, kind, b, value):
        pieces = value.reshape(NZ, 2, 16, BLK)
        for c in range(2):
            g_ref[layer, part, c, b * NZ : (b + 1) * NZ, kind * 16 : (kind + 1) * 16, :] = pieces[
                :, c
            ].astype(BF16)

    def early_grads(layer):
        for b in range(NX):
            rows = slice(b * BLK, (b + 1) * BLK)
            put_grad(layer, 0, 0, b, dot(ht_ref[layer, rows, :], dqkv_ref[0]))
            put_grad(layer, 0, 1, b, dot(ct_ref[rows, :], ob_ref[layer]))

    def late_grads(layer):
        for b in range(NX):
            left = ht_ref[layer, b * BLK : (b + 1) * BLK, :]
            put_grad(layer, 1, 0, b, dot(left, dqkv_ref[1]))
            put_grad(layer, 1, 1, b, dot(left, dqkv_ref[2]))

    def grads_core(layer, part):
        sem = GC + 2 * layer + part
        return start(
            remote(g_ref.at[layer, part, 1 - core], gc_ref.at[layer, part], sem, {"tok": mate})
        )

    def sum_core(layer, part, copy):
        copy.wait_recv()
        for j in (2, 1, 3, 0):
            rows = pl.ds(lax.rem(y + j, NY) * NZ, NZ)
            value = g_ref[layer, part, core, rows].astype(F32)
            value = value + gc_ref[layer, part, rows].astype(F32)
            g2_ref[layer, part, j] = value.astype(BF16)

    def grads_y(layer, part):
        sem = GY + 8 * layer + 4 * part
        return [
            start(remote(g2_ref.at[layer, part, j], gy_ref.at[layer, part, j], sem + j, ydev(j)))
            for j in (2, 1, 3)
        ]

    def grads_z(layer, part, copies):
        wait_all(copies)
        sem = GZ + 16 * layer + 8 * part
        later = []
        for j in (4, 3, 5, 2, 6, 1, 7, 0):
            at = lax.rem(z + j, NZ)
            value = g2_ref[layer, part, 0, at].astype(F32)
            for k in range(1, NY):
                value = value + gy_ref[layer, part, k, at].astype(F32)
            g3_ref[layer, part, j] = value.astype(BF16)
            if j:
                place = g3_ref.at[layer, part, j]
                later.append(start(remote(place, gz_ref.at[layer, part, j], sem + j, zdev(j))))
        return later

    def grads_end(layer, part, copies):
        wait_all(copies)
        value = g3_ref[layer, part, 0].astype(F32)
        for j in range(1, NZ):
            value = value + gz_ref[layer, part, j].astype(F32)
        value = value * GRAD_SCALE
        o_qkv, o_out = ((o_qkv1, o_out1), (o_qkv2, o_out2))[layer]
        if part == 0:
            o_qkv[0] = value[:16, :]
            o_out[...] = value[16:, :]
        else:
            o_qkv[1] = value[:16, :]
            o_qkv[2] = value[16:, :]

    loads[0].wait()
    normalize(0)
    loads[1].wait()
    keys_values(0)
    queries(0)
    pl.semaphore_wait(barrier, len(near))
    kv_copy = send_kv(0)
    for j in range(1, NY):
        pl.semaphore_signal(y_known, inc=1, device_id=ydev(j), device_id_type=MESH)
    turn_h(0)
    n0_ref[...] = jnp.zeros_like(n0_ref)
    kv_copy.wait_recv()
    attend(0)
    loads[2].wait()
    copies = ([], [])
    own = [None, None]
    for half in range(2):
        for j in (2, 1, 3, 0):
            part = dot(ob_ref[0], out1[:, half_cols(lax.rem(x + j, NX), half)])
            if j:
                copies[half].append(send_part(0, half, j, part))
            else:
                own[half] = part
    pl.semaphore_wait(y_known, NY - 1)
    pl.semaphore_signal(all_known, inc=1, device_id={"tok": mate}, device_id_type=MESH)
    indices()
    pl.semaphore_wait(all_known, 1)
    relays = []
    for half in range(2):
        wait_all(copies[half])
        y1 = (u_part(0, x, half) + total_part(0, half, own[half])).astype(BF16)
        relays.append(relay_out(0, half, s_ref, y1))
    for load in loads[3:]:
        load.wait()
    pull_back_out(1)
    turn_cot(1)
    copies = []
    for half in range(2):
        copies += spread(0, half, relay_in(0, half, r_ref, relays[half]))
    wait_all(copies)

    normalize(1)
    keys_values(1)
    kv_copy = send_kv(1)
    queries(1)
    turn_h(1)
    kv_copy.wait_recv()
    attend(1)
    attend_back(1, False, None)
    own, copies = send_dh(1)
    early_grads(1)
    cores_two = [grads_core(1, 0)]
    late_grads(1)
    cores_two.append(grads_core(1, 1))
    relays = []
    for half in range(2):
        wait_all(copies[half])
        if half == 0:
            mean = row_mean(1)
        du2 = finish_dh(1, half, total_part(1, half, own[half]), mean)
        relays.append(relay_out(1, half, rt_ref, du2))
    for part in range(2):
        sum_core(1, part, cores_two[part])
    copies = []
    for half in range(2):
        copies += spread(1, half, relay_in(1, half, st_ref, relays[half]))
    ys_two = [grads_y(1, part) for part in range(2)]
    wait_all(copies)

    pull_back_out(0)
    cores_one = []
    attend_back(0, True, cores_one)
    late_grads(0)
    cores_one.append(grads_core(0, 1))
    sum_core(0, 0, cores_one[0])
    ys_one = [grads_y(0, 0)]
    own, copies = send_dh(0)
    gain_copies = [start(remote(n0_ref, nc_ref, NC, {"tok": mate}))]
    sum_core(0, 1, cores_one[1])
    ys_one.append(grads_y(0, 1))
    zs_two = [grads_z(1, part, ys_two[part]) for part in range(2)]
    wait_all(gain_copies)
    n1_ref[...] = n0_ref[...] + nc_ref[...]
    gain_copies = [
        start(remote(n1_ref.at[lax.rem(y + j, NY)], ny_ref.at[j], NYS + j, ydev(j)))
        for j in range(1, NY)
    ]
    gathers = []
    for half in range(2):
        wait_all(copies[half])
        if half == 0:
            mean = row_mean(0)
        gathers += spread(2, half, finish_dh(0, half, total_part(2, half, own[half]), mean))
    wait_all(gain_copies)
    n2_ref[...] = n1_ref[y] + ny_ref[1] + ny_ref[2] + ny_ref[3]
    gain_copies = [start(remote(n2_ref, nz_ref.at[j], NZS + j, zdev(j))) for j in range(1, NZ)]
    zs_one = [grads_z(0, 0, ys_one[0])]
    for part in range(2):
        grads_end(1, part, zs_two[part])
    zs_one.append(grads_z(0, 1, ys_one[1]))
    wait_all(gain_copies)
    value = n2_ref[...]
    for j in range(1, NZ):
        value = value + nz_ref[j]
    n3_ref[...] = value
    gain_copies = [start(remote(n3_ref, nx_ref.at[j], NXS + j, xdev(j))) for j in range(1, NX)]
    wait_all(gathers)
    for b in range(NX):
        o_gin[:, b * BLK : (b + 1) * BLK] = gathered(2, b)
    wait_all(gain_copies)
    o_gain[...] = (n3_ref[...] + nx_ref[1] + nx_ref[2] + nx_ref[3]) * GRAD_SCALE
    for part in range(2):
        grads_end(0, part, zs_one[part])
    for copy in sends:
        copy.wait_send()


def deliver(
    gin, qkv1, out1, qkv2, out2, gains, o_gin, o_qkv1, o_out1, o_gain1, o_qkv2, o_out2, o_gain2
):
    pairs = ((gin, o_gin), (qkv1, o_qkv1), (out1, o_out1), (qkv2, o_qkv2), (out2, o_out2))
    for a, b in pairs:
        b[...] = a[...]
    at = lax.rem(lax.axis_index("tok"), NT // NX) * 16
    mine = pltpu.roll(gains[...], lax.rem(BLK - at, BLK), 1)
    o_gain1[...] = mine[0, :16]
    o_gain2[...] = mine[1, :16]


def scratch():
    def b16(*shape):
        return pltpu.VMEM(shape, BF16)

    def f32(*shape):
        return pltpu.VMEM(shape, F32)

    wide = NT * SLOTS
    width = NX * BLK
    return [
        b16(ROWS, width), b16(3, width, BLK), b16(BLK, width),
        b16(3, width, BLK), b16(BLK, width), b16(ROWS, width),
        b16(wide, ROWS), b16(ROWS, wide), b16(ROWS, wide), b16(wide, ROWS), f32(2, ROWS, ROWS),
        b16(2, ROWS, NX * BLK), b16(2, NX * BLK, ROWS), f32(2, ROWS, 1),
        b16(2, 2, 2, ROWS, BLK), b16(2, 2, BLK, ROWS), b16(2, 2, BLK, ROWS),
        b16(2, ROWS, BLK), b16(BLK, HEADS * ROWS), f32(2, 2, ROWS, HEADS * ROWS),
        b16(2, 2, ROWS, HEADS * ROWS), b16(BLK, ROWS), b16(2, ROWS, BLK),
        b16(ROWS, BLK), b16(BLK, ROWS), b16(2, ROWS, HEADS * ROWS), b16(HEADS * ROWS, BLK),
        b16(HEADS * ROWS, BLK), b16(BLK, ROWS), b16(3, ROWS, BLK), b16(2, 2, ROWS, BLK),
        b16(2, 2, ROWS, BLK), b16(NX * BLK, ROWS),
        b16(3, 2, NX, ROWS, HALF), b16(3, 2, NX, ROWS, HALF), f32(2, 8, ROWS), f32(2, NX, 8, ROWS),
        b16(2, 2, NT, SLOTS, HALF), b16(2, 2, NT, SLOTS, HALF), b16(3, 2, NX, ROWS, HALF),
        b16(2, 2, 2, NY * NZ, 32, BLK), b16(2, 2, NY * NZ, 32, BLK), b16(2, 2, NY, NZ, 32, BLK),
        b16(2, 2, NY, NZ, 32, BLK), b16(2, 2, NZ, 32, BLK), b16(2, 2, NZ, 32, BLK),
        f32(NX, 8, BLK), f32(NX, 8, BLK), f32(NX, 8, BLK), f32(NY, 8, BLK), f32(8, BLK),
        f32(NZ, 8, BLK), f32(8, BLK), f32(NX, 8, BLK),
        pltpu.SemaphoreType.DMA((NSEM,)), pltpu.SemaphoreType.DMA((NSEM,)),
        pltpu.SemaphoreType.DMA((6,)), pltpu.SemaphoreType.REGULAR, pltpu.SemaphoreType.REGULAR,
    ]


def local(
    tokens, gain_one, qkv_one, out_one, gain_two, qkv_two, out_two, hilbert_pos, scene, cotangent
):
    vmem = pl.BlockSpec(memory_space=pltpu.VMEM)
    hbm = pl.BlockSpec(memory_space=pl.ANY)
    grads = [
        jax.ShapeDtypeStruct((3, 16, BLK), F32),
        jax.ShapeDtypeStruct((16, BLK), F32),
    ]
    grad_input, qkv1, out1, qkv2, out2, gains = pl.pallas_call(
        kernel,
        out_shape=[
            jax.ShapeDtypeStruct((ROWS, NX * BLK), BF16),
            *grads,
            *grads,
            jax.ShapeDtypeStruct((8, BLK), F32),
        ],
        in_specs=[hbm, vmem, hbm, hbm, vmem, hbm, hbm, vmem, vmem, hbm],
        out_specs=[vmem] * 6,
        scratch_shapes=scratch(),
        compiler_params=pltpu.CompilerParams(
            collective_id=0, has_side_effects=True, vmem_limit_bytes=58 * 2**20
        ),
    )(
        tokens,
        gain_one.reshape(2 * NX, 128),
        qkv_one,
        out_one,
        gain_two.reshape(2 * NX, 128),
        qkv_two,
        out_two,
        hilbert_pos.reshape(2 * NT, 128),
        scene.reshape(2 * NT, 128),
        cotangent,
    )
    small = jax.ShapeDtypeStruct((16,), F32)
    grad_input, qkv1, out1, gain1, qkv2, out2, gain2 = pl.pallas_call(
        deliver,
        out_shape=[
            jax.ShapeDtypeStruct((ROWS, NX * BLK), BF16),
            *grads,
            small,
            *grads,
            small,
        ],
        in_specs=[vmem] * 6,
        out_specs=[vmem] * 7,
    )(grad_input, qkv1, out1, qkv2, out2, gains)
    return grad_input, qkv1, out1, gain1, qkv2, out2, gain2


def solution(mesh):
    in_specs = (
        P("tok", None),
        P(),
        P(None, None, "head"),
        P("head", None),
        P(),
        P(None, None, "head"),
        P("head", None),
        P(),
        P(),
        P("tok", None),
    )
    out_specs = (
        P("tok", None),
        P(None, "tok", "head"),
        P("tok", "head"),
        P("tok"),
        P(None, "tok", "head"),
        P("tok", "head"),
        P("tok"),
    )
    return jax.shard_map(local, mesh=mesh, in_specs=in_specs, out_specs=out_specs, check_vma=False)
```

```python
import jax
import jax.numpy as jnp
from jax import lax
from jax.experimental import pallas as pl
from jax.experimental.pallas import tpu as pltpu
from jax.sharding import PartitionSpec as P

MESH = pl.DeviceIdType.MESH
F32 = jnp.float32
BF16 = jnp.bfloat16
EPS = 1e-06
ROWS = 256
BLK = 256
NX = 4
NT = 64
NY = 4
NZ = 8
HEADS = 4
HD = 64
SLOTS = 8
GRAD_SCALE = 1.0 / 128.0

HALF = 128

GROUPS = ((0, 16), (16, 16), (32, 32))

KV = 0
BACK = 2
A2A = 4
GC = 156
ROWSUM = 12
NC = 20
NYS = 20
NXS = 24
NZS = 28
RS = 36
AG = 60
GY = 84
GZ = 108
NSEM = 162


def dot(a, b):
    return lax.dot_general(a, b, (((1,), (0,)), ((), ())), preferred_element_type=F32)


def dot_nt(a, b):
    return lax.dot_general(a, b, (((1,), (1,)), ((), ())), preferred_element_type=F32)


def kernel(
    tokens_in, gain1, qkv1_in, out1_in, gain2, qkv2_in, out2_in, hpos, scene, cot_in,
    o_gin, o_qkv1, o_out1, o_qkv2, o_out2, o_gain,
    tokens, qkv1, out1, qkv2, out2, cot,
    s_ref, st_ref, r_ref, rt_ref, bias_ref,
    h_ref, ht_ref, rinv_ref, kv_ref, kt_ref, vt_ref, q_ref, qt_ref, p_ref, pb_ref, obt_ref, ob_ref,
    do_ref, dot_ref, ds_ref, qstk_ref, dostk_ref, dqt_ref, dqkv_ref, kvs_ref, kvr_ref, ct_ref,
    rss_ref, rsr_ref, ms_ref, mr_ref, as_ref, ar_ref, ag_ref,
    g_ref, gc_ref, g2_ref, gy_ref, g3_ref, gz_ref, e2_ref, ez_ref, e3_ref, ey_ref,
    n0_ref, nc_ref, n1_ref, ny_ref, n2_ref, nz_ref, n3_ref, nx_ref,
    ssem, rsem, lsem, y_known, all_known,
):
    t = lax.axis_index("tok")
    x = lax.axis_index("head")
    core = lax.rem(t, 2)
    z = lax.rem(t // 2, NZ)
    y = t // (2 * NZ)
    mate = t + 1 - 2 * core
    gains, qkvs, outs = (gain1, gain2), (qkv1, qkv2), (out1, out2)

    def xdev(j):
        return {"head": lax.rem(x + j, NX)}

    def ydev(j):
        return {"tok": (lax.rem(y + j, NY) * NZ + z) * 2 + core}

    def zdev(j):
        return {"tok": (y * NZ + lax.rem(z + j, NZ)) * 2 + core}

    def remote(src, dst, sem, dev):
        return pltpu.make_async_remote_copy(
            src_ref=src, dst_ref=dst, send_sem=ssem.at[sem], recv_sem=rsem.at[sem],
            device_id=dev, device_id_type=MESH,
        )

    loads = [
        pltpu.make_async_copy(source, target, lsem.at[i])
        for i, (source, target) in enumerate(
            (
                (tokens_in, tokens),
                (qkv1_in, qkv1),
                (out1_in, out1),
                (qkv2_in, qkv2),
                (out2_in, out2),
                (cot_in, cot),
            )
        )
    ]
    loads[0].start()
    loads[1].start()
    barrier = pltpu.get_barrier_semaphore()

    near = [{"tok": mate}]
    near += [xdev(j) for j in range(1, NX)]
    near += [ydev(j) for j in range(1, NY)]
    near += [zdev(j) for j in range(1, NZ)]
    for dev in near:
        pl.semaphore_signal(barrier, inc=1, device_id=dev, device_id_type=MESH)

    sends = []

    def start(copy):
        copy.start()
        sends.append(copy)
        return copy

    def gathered(phase, b):
        return jnp.concatenate([ag_ref[phase, 0, b], ag_ref[phase, 1, b]], axis=1)

    def u_block(layer, b):
        if layer == 0:
            return tokens[:, b * BLK : (b + 1) * BLK].astype(F32)
        return gathered(0, b).astype(F32)

    def half_cols(at, half):
        return pl.ds(pl.multiple_of(at * BLK + half * HALF, HALF), HALF)

    def u_part(layer, at, half):
        if layer == 0:
            return tokens[:, half_cols(at, half)].astype(F32)
        return ag_ref[0, half, at].astype(F32)

    def gain_part(layer, at, half):
        return gains[layer][pl.ds(2 * at + half, 1), :]

    def cot_block(layer, b):
        return cot[:, b * BLK : (b + 1) * BLK] if layer == 1 else gathered(1, b)

    def cot_part(layer, half):
        if layer == 1:
            return cot[:, half_cols(x, half)].astype(F32)
        return ag_ref[1, half, x].astype(F32)

    def wide_row(ref, at):
        return jnp.concatenate([ref[pl.ds(2 * at, 1), :], ref[pl.ds(2 * at + 1, 1), :]], axis=1)

    def indices():
        lane_lt = lax.broadcasted_iota(jnp.int32, (ROWS, ROWS), 0) < lax.broadcasted_iota(
            jnp.int32, (ROWS, ROWS), 1
        )
        tri = jnp.where(lane_lt, 1.0, 0.0).astype(BF16)
        slot = lax.broadcasted_iota(jnp.int32, (NT * SLOTS, ROWS), 0).astype(F32)
        dev = lax.broadcasted_iota(jnp.int32, (NT, ROWS), 0)
        lane = lax.broadcasted_iota(jnp.int32, (NT, ROWS), 1).astype(F32)
        own = wide_row(hpos, t) // ROWS
        hit = jnp.where(dev == own, 1.0, 0.0)
        before = dot(hit.astype(BF16), tri)
        send_id = jnp.sum(hit * (before + dev.astype(F32) * SLOTS), axis=0, keepdims=True)
        s = jnp.where(slot == send_id, 1.0, 0.0)
        s_ref[...] = s.astype(BF16)
        st_ref[...] = s.T.astype(BF16)
        every = jnp.concatenate([hpos[0::2, :], hpos[1::2, :]], axis=1)
        place = lax.rem(every, ROWS).astype(F32)
        mine = jnp.where(every // ROWS == t, 1.0, 0.0)
        rank = dot(mine.astype(BF16), tri)
        recv_id = jnp.zeros((1, ROWS), F32)
        for k in range(SLOTS):
            chosen = mine * jnp.where(rank == k, 1.0, 0.0)
            row = jnp.sum(chosen * (place + 1.0), axis=1, keepdims=True) - 1.0
            found = jnp.where(row == lane, dev.astype(F32) * SLOTS + k, 0.0)
            recv_id = recv_id + jnp.sum(found, axis=0, keepdims=True)
        r = jnp.where(slot == recv_id, 1.0, 0.0)
        rt_ref[...] = r.astype(BF16)
        r_ref[...] = r.T.astype(BF16)
        ids = wide_row(scene, t).astype(F32)
        for half, source in ((0, t), (1, mate)):
            row = wide_row(scene, source).astype(F32)
            col = jnp.broadcast_to(row, (128, ROWS)).T[:, :1]
            bias_ref[half] = jnp.where(col == ids, 0.0, -1e30)

    def normalize(layer):
        total = jnp.zeros((ROWS, 1), F32)
        for b in range(NX):
            ub = u_block(layer, b)
            total = total + jnp.sum(ub * ub, axis=1, keepdims=True)
        rinv = lax.rsqrt(total * (1.0 / (NX * BLK)) + EPS)
        rinv_ref[layer] = rinv
        for b in range(NX):
            hb = u_block(layer, b) * rinv * wide_row(gains[layer], b)
            h_ref[layer, :, b * BLK : (b + 1) * BLK] = hb.astype(BF16)

    def keys_values(layer):
        h = h_ref[layer]
        kv_ref[layer, 0, 0] = dot(h, qkvs[layer][1]).astype(BF16)
        kv_ref[layer, 0, 1] = dot(h, qkvs[layer][2]).astype(BF16)

    def send_kv(layer):
        return start(
            remote(kv_ref.at[layer, 0], kv_ref.at[layer, 1], KV + layer, {"tok": mate})
        )

    row_head = lax.broadcasted_iota(jnp.int32, (BLK, ROWS), 0) // HD
    lane_head = lax.broadcasted_iota(jnp.int32, (ROWS, BLK), 1) // HD

    def queries(layer):
        q = dot(h_ref[layer], qkvs[layer][0]).astype(BF16).astype(F32) * 0.125
        q_ref[layer] = q.astype(BF16)
        qt = q.T
        for n in range(HEADS):
            qt_ref[:, n * ROWS : (n + 1) * ROWS] = jnp.where(row_head == n, qt, 0.0).astype(BF16)

    def attend(layer):
        for half in range(2):
            kt_ref[layer, half] = kv_ref[layer, half, 0].T
            vt_ref[layer, half] = kv_ref[layer, half, 1].T
        for n in range(HEADS):
            cols = slice(n * ROWS, (n + 1) * ROWS)
            rows = slice(n * HD, (n + 1) * HD)
            e = []
            for half in range(2):
                scores = dot(kv_ref[layer, half, 0], qt_ref[:, cols])
                if layer == 1:
                    scores = scores + bias_ref[half]
                e.append(jnp.exp(scores))
            total = jnp.sum(e[0], axis=0, keepdims=True) + jnp.sum(e[1], axis=0, keepdims=True)
            inv = 1.0 / total
            mixed = jnp.zeros((HD, ROWS), F32)
            for half in range(2):
                p = e[half] * inv
                p_ref[layer, half, :, cols] = p
                pb = p.astype(BF16)
                pb_ref[layer, half, :, cols] = pb
                mixed = mixed + dot(vt_ref[layer, half, rows, :], pb)
            obt_ref[rows, :] = mixed.astype(BF16)
        ob_ref[layer] = obt_ref[...].T

    def turn_h(layer):
        for b in range(NX):
            ht_ref[layer, b * BLK : (b + 1) * BLK, :] = h_ref[layer, :, b * BLK : (b + 1) * BLK].T

    def pull_back_out(layer):
        acc = jnp.zeros((ROWS, BLK), F32)
        for b in range(NX):
            acc = acc + dot_nt(cot_block(layer, b), outs[layer][:, b * BLK : (b + 1) * BLK])
        do = acc.astype(BF16)
        do_ref[...] = do
        dot_ref[...] = do.T
        for n in range(HEADS):
            dostk_ref[n * ROWS : (n + 1) * ROWS, :] = jnp.where(
                lane_head == n, do.astype(F32), 0.0
            ).astype(BF16)

    def attend_back(layer, meanwhile):
        q = q_ref[layer].astype(F32)
        dt = dot_ref[...].astype(F32)
        for n in range(HEADS):
            cols = slice(n * ROWS, (n + 1) * ROWS)
            rows = slice(n * HD, (n + 1) * HD)
            qstk_ref[n * ROWS : (n + 1) * ROWS, :] = jnp.where(lane_head == n, q, 0.0).astype(BF16)
            only = jnp.where(row_head == n, dt, 0.0).astype(BF16)
            dp = [dot(kv_ref[layer, half, 1], only) for half in range(2)]
            p = [p_ref[layer, half, :, cols] for half in range(2)]
            r = jnp.sum(dp[0] * p[0], axis=0, keepdims=True) + jnp.sum(
                dp[1] * p[1], axis=0, keepdims=True
            )
            dq = jnp.zeros((HD, ROWS), F32)
            for half in range(2):
                ds = (p[half] * (dp[half] - r)).astype(BF16)
                ds_ref[half, :, cols] = ds
                dq = dq + dot(kt_ref[layer, half, rows, :], ds)
            dqt_ref[rows, :] = (dq * 0.125).astype(BF16)
        kvs_ref[layer, 0] = dot(ds_ref[1], qstk_ref[...]).astype(BF16)
        kvs_ref[layer, 1] = dot(pb_ref[layer, 1], dostk_ref[...]).astype(BF16)
        copy = start(
            remote(kvs_ref.at[layer], kvr_ref.at[layer], BACK + layer, {"tok": mate})
        )
        dqkv_ref[0] = dqt_ref[...].T
        dk = dot(ds_ref[0], qstk_ref[...])
        dv = dot(pb_ref[layer, 0], dostk_ref[...])
        meanwhile()
        copy.wait_recv()
        dqkv_ref[1] = (dk + kvr_ref[layer, 0].astype(F32)).astype(BF16)
        dqkv_ref[2] = (dv + kvr_ref[layer, 1].astype(F32)).astype(BF16)

    def dh_part(layer, at, half):
        rows = half_cols(at, half)
        acc = dot_nt(dqkv_ref[0], qkvs[layer][0, rows, :])
        acc = acc + dot_nt(dqkv_ref[1], qkvs[layer][1, rows, :])
        return acc + dot_nt(dqkv_ref[2], qkvs[layer][2, rows, :])

    def send_part(phase, half, j, part):
        rss_ref[phase, half, j] = part.astype(BF16)
        sem = RS + 8 * phase + 4 * half + j
        return start(remote(rss_ref.at[phase, half, j], rsr_ref.at[phase, half, j], sem, xdev(j)))

    def send_dh(layer):
        phase = 2 - layer
        sums = jnp.zeros((ROWS, 1), F32)
        copies = ([], [])
        own = [None, None]
        rinv = rinv_ref[layer]
        for half in range(2):
            for j in (2, 1, 3, 0):
                at = lax.rem(x + j, NX)
                part = dh_part(layer, at, half)
                if j:
                    copies[half].append(send_part(phase, half, j, part))
                else:
                    own[half] = part
                weighted = part * u_part(layer, at, half)
                sums = sums + jnp.sum(
                    weighted * gain_part(layer, at, half), axis=1, keepdims=True
                )
                n0_ref[at, layer : layer + 1, half * HALF : (half + 1) * HALF] = jnp.sum(
                    weighted * rinv, axis=0, keepdims=True
                )
        ms_ref[layer] = jnp.broadcast_to(sums, (ROWS, 128)).T[:8, :]
        for j in (2, 1, 3):
            sem = ROWSUM + 4 * layer + j
            copies[0].append(start(remote(ms_ref.at[layer], mr_ref.at[layer, j], sem, xdev(j))))
        return own, copies

    def row_mean(layer):
        sums = ms_ref[layer]
        for j in range(1, NX):
            sums = sums + mr_ref[layer, j]
        return jnp.broadcast_to(sums[:1, :], (128, ROWS)).T[:, :1] * (1.0 / (NX * BLK))

    def wait_all(copies):
        for copy in copies:
            copy.wait_recv()

    def total_part(phase, half, own):
        for j in range(1, NX):
            own = own + rsr_ref[phase, half, j].astype(F32)
        return own

    def finish_dh(layer, half, dh, mean):
        u = u_part(layer, x, half)
        rinv = rinv_ref[layer]
        scaled = dh * gain_part(layer, x, half)
        du = cot_part(layer, half) + rinv * (scaled - u * rinv * rinv * mean)
        return du.astype(BF16)

    def relay_out(way, half, table, chunk):
        packed = dot(table[...], chunk).reshape(NT, SLOTS, HALF)
        as_ref[way, half] = packed.astype(BF16)
        ar_ref[way, half, t] = as_ref[way, half, t]
        sem = A2A + 2 * way + half

        def push(j, carry):
            to = lax.rem(t + j, NT)
            remote(as_ref.at[way, half, to], ar_ref.at[way, half, t], sem, {"tok": to}).start()
            return carry

        lax.fori_loop(1, NT, push, 0)
        every = pl.ds(0, NT - 1)
        copy = remote(
            as_ref.at[way, half, every], ar_ref.at[way, half, every], sem, {"tok": mate}
        )
        sends.append(copy)
        return copy

    def relay_in(way, half, table, copy):
        copy.wait_recv()
        packed = ar_ref[way, half].astype(F32).reshape(NT * SLOTS, HALF).astype(BF16)
        return dot(table[...], packed).astype(BF16)

    def spread(phase, half, chunk):
        ag_ref[phase, half, x] = chunk
        place = ag_ref.at[phase, half, x]
        sem = AG + 8 * phase + 4 * half
        return [start(remote(place, place, sem + j, xdev(j))) for j in (2, 1, 3)]

    def turn_cot():
        for half in range(2):
            for b in range(NX):
                at = b * BLK + half * HALF
                ct_ref[half, b * HALF : (b + 1) * HALF, :] = cot[:, at : at + HALF].T

    def put_grad(layer, kind, chip, value):
        n = value.shape[0] // 32
        pieces = value.reshape(n, 2, 16, BLK)
        for c in range(2):
            g_ref[layer, c, chip : chip + n, kind * 16 : (kind + 1) * 16, :] = pieces[:, c].astype(
                BF16
            )

    def out_grads(layer, half):
        for b in range(NX):
            if layer == 0:
                left = ag_ref[1, half, b].T
            else:
                left = ct_ref[half, b * HALF : (b + 1) * HALF, :]
            put_grad(layer, 0, b * NZ + half * (NZ // 2), dot(left, ob_ref[layer]))

    def qkv_grads(layer, kinds):
        for b in range(NX):
            left = ht_ref[layer, b * BLK : (b + 1) * BLK, :]
            for kind in kinds:
                put_grad(layer, kind + 1, b * NZ, dot(left, dqkv_ref[kind]))

    def rows_of(layer, group):
        first, count = GROUPS[group]
        return pl.ds(first, count)

    def grads_core(layer, group):
        rows = rows_of(layer, group)
        return start(
            remote(
                g_ref.at[layer, 1 - core, :, rows],
                gc_ref.at[layer, :, rows],
                GC + 3 * layer + group,
                {"tok": mate},
            )
        )

    def grads_y(layer, group, copy):
        copy.wait_recv()
        rows = rows_of(layer, group)
        sem = GY + 12 * layer + 4 * group
        copies = []
        for j in (2, 1, 3, 0):
            chips = pl.ds(lax.rem(y + j, NY) * NZ, NZ)
            value = g_ref[layer, core, chips, rows].astype(F32)
            value = value + gc_ref[layer, chips, rows].astype(F32)
            g2_ref[layer, j, :, rows] = value.astype(BF16)
            if j:
                place = g2_ref.at[layer, j, :, rows]
                copies.append(
                    start(remote(place, gy_ref.at[layer, j, :, rows], sem + j, ydev(j)))
                )
        return copies

    def grads_z(layer, group, copies):
        wait_all(copies)
        rows = rows_of(layer, group)
        sem = GZ + 24 * layer + 8 * group
        later = []
        for j in (4, 3, 5, 2, 6, 1, 7, 0):
            at = lax.rem(z + j, NZ)
            value = g2_ref[layer, 0, at, rows].astype(F32)
            for k in range(1, NY):
                value = value + gy_ref[layer, k, at, rows].astype(F32)
            g3_ref[layer, j, rows] = value.astype(BF16)
            if j:
                place = g3_ref.at[layer, j, rows]
                later.append(start(remote(place, gz_ref.at[layer, j, rows], sem + j, zdev(j))))
        return later

    def grads_end(layer, group, copies):
        wait_all(copies)
        rows = rows_of(layer, group)
        value = g3_ref[layer, 0, rows].astype(F32)
        for j in range(1, NZ):
            value = value + gz_ref[layer, j, rows].astype(F32)
        value = value * GRAD_SCALE
        o_qkv = (o_qkv1, o_qkv2)[layer]
        first, count = GROUPS[group]
        for i in range(count // 16):
            o_qkv[first // 16 + i - 1] = value[i * 16 : (i + 1) * 16, :]

    def out_z(layer, copy):
        copy.wait_recv()
        copies = []
        for j in (4, 3, 5, 2, 6, 1, 7, 0):
            at = lax.rem(z + j, NZ)
            for k in range(NY):
                chip = k * NZ + at
                value = g_ref[layer, core, chip, 0:16].astype(F32)
                value = value + gc_ref[layer, chip, 0:16].astype(F32)
                e2_ref[layer, j, k] = value.astype(BF16)
            if j:
                place = e2_ref.at[layer, j]
                copies.append(
                    start(remote(place, ez_ref.at[layer, j], GZ + 24 * layer + j, zdev(j)))
                )
        return copies

    def out_y(layer, copies):
        wait_all(copies)
        later = []
        for j in (2, 1, 3, 0):
            at = lax.rem(y + j, NY)
            value = e2_ref[layer, 0, at].astype(F32)
            for k in range(1, NZ):
                value = value + ez_ref[layer, k, at].astype(F32)
            e3_ref[layer, j] = value.astype(BF16)
            if j:
                place = e3_ref.at[layer, j]
                later.append(
                    start(remote(place, ey_ref.at[layer, j], GY + 12 * layer + j, ydev(j)))
                )
        return later

    def out_end(layer, copies):
        wait_all(copies)
        value = e3_ref[layer, 0].astype(F32)
        for j in range(1, NY):
            value = value + ey_ref[layer, j].astype(F32)
        (o_out1, o_out2)[layer][...] = value * GRAD_SCALE

    def hop_one(layer, group, copy):
        return grads_y(layer, group, copy) if group else out_z(layer, copy)

    def hop_two(layer, group, copies):
        return grads_z(layer, group, copies) if group else out_y(layer, copies)

    def hops_end(layer, group, copies):
        if group:
            grads_end(layer, group, copies)
        else:
            out_end(layer, copies)

    loads[0].wait()
    normalize(0)
    loads[1].wait()
    loads[2].start()
    keys_values(0)
    queries(0)
    pl.semaphore_wait(barrier, len(near))
    kv_copy = send_kv(0)
    for j in range(1, NY):
        pl.semaphore_signal(y_known, inc=1, device_id=ydev(j), device_id_type=MESH)
    turn_h(0)
    n0_ref[...] = jnp.zeros_like(n0_ref)
    kv_copy.wait_recv()
    for load in loads[3:]:
        load.start()
    attend(0)
    loads[2].wait()
    copies = ([], [])
    own = [None, None]
    for half in range(2):
        for j in (2, 1, 3, 0):
            part = dot(ob_ref[0], out1[:, half_cols(lax.rem(x + j, NX), half)])
            if j:
                copies[half].append(send_part(0, half, j, part))
            else:
                own[half] = part
    pl.semaphore_wait(y_known, NY - 1)
    pl.semaphore_signal(all_known, inc=1, device_id={"tok": mate}, device_id_type=MESH)
    indices()
    pl.semaphore_wait(all_known, 1)
    relays = []
    for half in range(2):
        wait_all(copies[half])
        y1 = (u_part(0, x, half) + total_part(0, half, own[half])).astype(BF16)
        relays.append(relay_out(0, half, s_ref, y1))
    for load in loads[3:]:
        load.wait()
    pull_back_out(1)
    turn_cot()
    copies = []
    for half in range(2):
        copies += spread(0, half, relay_in(0, half, r_ref, relays[half]))
    wait_all(copies)

    normalize(1)
    keys_values(1)
    kv_copy = send_kv(1)
    queries(1)
    turn_h(1)
    kv_copy.wait_recv()
    attend(1)
    cores_two = []

    def meanwhile_two():
        for half in range(2):
            out_grads(1, half)
        cores_two.append(grads_core(1, 0))

    attend_back(1, meanwhile_two)
    own, copies = send_dh(1)
    qkv_grads(1, (0,))
    cores_two.append(grads_core(1, 1))
    ys_two = [hop_one(1, 0, cores_two[0])]
    qkv_grads(1, (1, 2))
    cores_two.append(grads_core(1, 2))
    ys_two.append(hop_one(1, 1, cores_two[1]))
    relays = []
    for half in range(2):
        wait_all(copies[half])
        if half == 0:
            mean = row_mean(1)
        du2 = finish_dh(1, half, total_part(1, half, own[half]), mean)
        relays.append(relay_out(1, half, rt_ref, du2))
    copies = []
    for half in range(2):
        copies.append(spread(1, half, relay_in(1, half, st_ref, relays[half])))
    ys_two.append(hop_one(1, 2, cores_two[2]))
    zs_two = [hop_two(1, group, ys_two[group]) for group in range(2)]

    for half in range(2):
        wait_all(copies[half])
        out_grads(0, half)
    cores_one = [grads_core(0, 0)]
    pull_back_out(0)
    ys_one = []

    def meanwhile_one():
        qkv_grads(0, (0,))
        cores_one.append(grads_core(0, 1))
        ys_one.append(hop_one(0, 0, cores_one[0]))

    attend_back(0, meanwhile_one)
    qkv_grads(0, (1, 2))
    cores_one.append(grads_core(0, 2))
    ys_one.append(hop_one(0, 1, cores_one[1]))
    zs_two.append(hop_two(1, 2, ys_two[2]))
    own, copies = send_dh(0)
    gain_copies = [start(remote(n0_ref, nc_ref, NC, {"tok": mate}))]
    ys_one.append(hop_one(0, 2, cores_one[2]))
    wait_all(gain_copies)
    n1_ref[...] = n0_ref[...] + nc_ref[...]
    gain_copies = [
        start(remote(n1_ref.at[lax.rem(y + j, NY)], ny_ref.at[j], NYS + j, ydev(j)))
        for j in range(1, NY)
    ]
    for group in range(3):
        hops_end(1, group, zs_two[group])
    zs_one = [hop_two(0, group, ys_one[group]) for group in range(2)]
    gathers = []
    for half in range(2):
        wait_all(copies[half])
        if half == 0:
            mean = row_mean(0)
        gathers += spread(2, half, finish_dh(0, half, total_part(2, half, own[half]), mean))
    wait_all(gain_copies)
    n2_ref[...] = n1_ref[y] + ny_ref[1] + ny_ref[2] + ny_ref[3]
    gain_copies = [start(remote(n2_ref, nz_ref.at[j], NZS + j, zdev(j))) for j in range(1, NZ)]
    zs_one.append(hop_two(0, 2, ys_one[2]))
    wait_all(gain_copies)
    value = n2_ref[...]
    for j in range(1, NZ):
        value = value + nz_ref[j]
    n3_ref[...] = value
    gain_copies = [start(remote(n3_ref, nx_ref.at[j], NXS + j, xdev(j))) for j in range(1, NX)]
    wait_all(gathers)
    for b in range(NX):
        o_gin[:, b * BLK : (b + 1) * BLK] = gathered(2, b)
    wait_all(gain_copies)
    o_gain[...] = (n3_ref[...] + nx_ref[1] + nx_ref[2] + nx_ref[3]) * GRAD_SCALE
    for group in range(3):
        hops_end(0, group, zs_one[group])
    for copy in sends:
        copy.wait_send()


def deliver(
    gin, qkv1, out1, qkv2, out2, gains, o_gin, o_qkv1, o_out1, o_gain1, o_qkv2, o_out2, o_gain2
):
    pairs = ((gin, o_gin), (qkv1, o_qkv1), (out1, o_out1), (qkv2, o_qkv2), (out2, o_out2))
    for a, b in pairs:
        b[...] = a[...]
    at = lax.rem(lax.axis_index("tok"), NT // NX) * 16
    mine = pltpu.roll(gains[...], lax.rem(BLK - at, BLK), 1)
    o_gain1[...] = mine[0, :16]
    o_gain2[...] = mine[1, :16]


def scratch():
    def b16(*shape):
        return pltpu.VMEM(shape, BF16)

    def f32(*shape):
        return pltpu.VMEM(shape, F32)

    wide = NT * SLOTS
    width = NX * BLK
    return [
        b16(ROWS, width), b16(3, width, BLK), b16(BLK, width),
        b16(3, width, BLK), b16(BLK, width), b16(ROWS, width),
        b16(wide, ROWS), b16(ROWS, wide), b16(ROWS, wide), b16(wide, ROWS), f32(2, ROWS, ROWS),
        b16(2, ROWS, NX * BLK), b16(2, NX * BLK, ROWS), f32(2, ROWS, 1),
        b16(2, 2, 2, ROWS, BLK), b16(2, 2, BLK, ROWS), b16(2, 2, BLK, ROWS),
        b16(2, ROWS, BLK), b16(BLK, HEADS * ROWS), f32(2, 2, ROWS, HEADS * ROWS),
        b16(2, 2, ROWS, HEADS * ROWS), b16(BLK, ROWS), b16(2, ROWS, BLK),
        b16(ROWS, BLK), b16(BLK, ROWS), b16(2, ROWS, HEADS * ROWS), b16(HEADS * ROWS, BLK),
        b16(HEADS * ROWS, BLK), b16(BLK, ROWS), b16(3, ROWS, BLK), b16(2, 2, ROWS, BLK),
        b16(2, 2, ROWS, BLK), b16(2, NX * HALF, ROWS),
        b16(3, 2, NX, ROWS, HALF), b16(3, 2, NX, ROWS, HALF), f32(2, 8, ROWS), f32(2, NX, 8, ROWS),
        b16(2, 2, NT, SLOTS, HALF), b16(2, 2, NT, SLOTS, HALF), b16(3, 2, NX, ROWS, HALF),
        b16(2, 2, NY * NZ, 64, BLK), b16(2, NY * NZ, 64, BLK), b16(2, NY, NZ, 64, BLK),
        b16(2, NY, NZ, 64, BLK), b16(2, NZ, 64, BLK), b16(2, NZ, 64, BLK),
        b16(2, NZ, NY, 16, BLK), b16(2, NZ, NY, 16, BLK), b16(2, NY, 16, BLK), b16(2, NY, 16, BLK),
        f32(NX, 8, BLK), f32(NX, 8, BLK), f32(NX, 8, BLK), f32(NY, 8, BLK), f32(8, BLK),
        f32(NZ, 8, BLK), f32(8, BLK), f32(NX, 8, BLK),
        pltpu.SemaphoreType.DMA((NSEM,)), pltpu.SemaphoreType.DMA((NSEM,)),
        pltpu.SemaphoreType.DMA((6,)), pltpu.SemaphoreType.REGULAR, pltpu.SemaphoreType.REGULAR,
    ]


def local(
    tokens, gain_one, qkv_one, out_one, gain_two, qkv_two, out_two, hilbert_pos, scene, cotangent
):
    vmem = pl.BlockSpec(memory_space=pltpu.VMEM)
    hbm = pl.BlockSpec(memory_space=pl.ANY)
    grads = [
        jax.ShapeDtypeStruct((3, 16, BLK), F32),
        jax.ShapeDtypeStruct((16, BLK), F32),
    ]
    grad_input, qkv1, out1, qkv2, out2, gains = pl.pallas_call(
        kernel,
        out_shape=[
            jax.ShapeDtypeStruct((ROWS, NX * BLK), BF16),
            *grads,
            *grads,
            jax.ShapeDtypeStruct((8, BLK), F32),
        ],
        in_specs=[hbm, vmem, hbm, hbm, vmem, hbm, hbm, vmem, vmem, hbm],
        out_specs=[vmem] * 6,
        scratch_shapes=scratch(),
        compiler_params=pltpu.CompilerParams(
            collective_id=0, has_side_effects=True, vmem_limit_bytes=58 * 2**20
        ),
    )(
        tokens,
        gain_one.reshape(2 * NX, 128),
        qkv_one,
        out_one,
        gain_two.reshape(2 * NX, 128),
        qkv_two,
        out_two,
        hilbert_pos.reshape(2 * NT, 128),
        scene.reshape(2 * NT, 128),
        cotangent,
    )
    small = jax.ShapeDtypeStruct((16,), F32)
    grad_input, qkv1, out1, gain1, qkv2, out2, gain2 = pl.pallas_call(
        deliver,
        out_shape=[
            jax.ShapeDtypeStruct((ROWS, NX * BLK), BF16),
            *grads,
            small,
            *grads,
            small,
        ],
        in_specs=[vmem] * 6,
        out_specs=[vmem] * 7,
    )(grad_input, qkv1, out1, qkv2, out2, gains)
    return grad_input, qkv1, out1, gain1, qkv2, out2, gain2


def solution(mesh):
    in_specs = (
        P("tok", None),
        P(),
        P(None, None, "head"),
        P("head", None),
        P(),
        P(None, None, "head"),
        P("head", None),
        P(),
        P(),
        P("tok", None),
    )
    out_specs = (
        P("tok", None),
        P(None, "tok", "head"),
        P("tok", "head"),
        P("tok"),
        P(None, "tok", "head"),
        P("tok", "head"),
        P("tok"),
    )
    return jax.shard_map(local, mesh=mesh, in_specs=in_specs, out_specs=out_specs, check_vma=False)
```

```python
import jax
import jax.numpy as jnp
from jax import lax
from jax.experimental import pallas as pl
from jax.experimental.pallas import tpu as pltpu
from jax.sharding import PartitionSpec as P

MESH = pl.DeviceIdType.MESH
F32 = jnp.float32
BF16 = jnp.bfloat16
EPS = 1e-06
ROWS = 256
BLK = 256
NX = 4
NT = 64
NY = 4
NZ = 8
HEADS = 4
HD = 64
SLOTS = 8
GRAD_SCALE = 1.0 / 128.0

HALF = 128

GROUPS = ((0, 16), (16, 16), (32, 32))

KV = 0
BACK = 2
A2A = 4
GC = 156
ROWSUM = 12
NC = 20
NYS = 20
NXS = 24
NZS = 28
RS = 36
AG = 60
GY = 84
GZ = 108
NSEM = 162


def dot(a, b):
    return lax.dot_general(a, b, (((1,), (0,)), ((), ())), preferred_element_type=F32)


def dot_nt(a, b):
    return lax.dot_general(a, b, (((1,), (1,)), ((), ())), preferred_element_type=F32)


def kernel(
    tokens_in, gain1, qkv1_in, out1_in, gain2, qkv2_in, out2_in, hpos, scene, cot_in,
    o_gin, o_qkv1, o_out1, o_qkv2, o_out2, o_gain,
    tokens, qkv1, out1, qkv2, out2, cot,
    s_ref, st_ref, r_ref, rt_ref, bias_ref,
    h_ref, ht_ref, rinv_ref, kv_ref, kt_ref, vt_ref, q_ref, qt_ref, p_ref, pb_ref, obt_ref, ob_ref,
    do_ref, dot_ref, ds_ref, qstk_ref, dostk_ref, dqt_ref, dqkv_ref, kvs_ref, kvr_ref, ct_ref,
    rss_ref, rsr_ref, ms_ref, mr_ref, as_ref, ar_ref, ag_ref,
    g_ref, gc_ref, g2_ref, gy_ref, g3_ref, gz_ref, e2_ref, ez_ref, e3_ref, ey_ref,
    n0_ref, nc_ref, n1_ref, ny_ref, n2_ref, nz_ref, n3_ref, nx_ref,
    ssem, rsem, lsem, y_known, all_known,
):
    t = lax.axis_index("tok")
    x = lax.axis_index("head")
    core = lax.rem(t, 2)
    z = lax.rem(t // 2, NZ)
    y = t // (2 * NZ)
    mate = t + 1 - 2 * core
    gains, qkvs, outs = (gain1, gain2), (qkv1, qkv2), (out1, out2)

    def xdev(j):
        return {"head": lax.rem(x + j, NX)}

    def ydev(j):
        return {"tok": (lax.rem(y + j, NY) * NZ + z) * 2 + core}

    def zdev(j):
        return {"tok": (y * NZ + lax.rem(z + j, NZ)) * 2 + core}

    def remote(src, dst, sem, dev):
        return pltpu.make_async_remote_copy(
            src_ref=src, dst_ref=dst, send_sem=ssem.at[sem], recv_sem=rsem.at[sem],
            device_id=dev, device_id_type=MESH,
        )

    loads = [
        pltpu.make_async_copy(source, target, lsem.at[i])
        for i, (source, target) in enumerate(
            (
                (tokens_in, tokens),
                (qkv1_in, qkv1),
                (out1_in, out1),
                (qkv2_in, qkv2),
                (out2_in, out2),
                (cot_in, cot),
            )
        )
    ]
    loads[0].start()
    loads[1].start()
    barrier = pltpu.get_barrier_semaphore()

    near = [{"tok": mate}]
    near += [xdev(j) for j in range(1, NX)]
    near += [ydev(j) for j in range(1, NY)]
    near += [zdev(j) for j in range(1, NZ)]
    for dev in near:
        pl.semaphore_signal(barrier, inc=1, device_id=dev, device_id_type=MESH)

    sends = []

    def start(copy):
        copy.start()
        sends.append(copy)
        return copy

    def gathered(phase, b):
        return jnp.concatenate([ag_ref[phase, 0, b], ag_ref[phase, 1, b]], axis=1)

    def u_block(layer, b):
        if layer == 0:
            return tokens[:, b * BLK : (b + 1) * BLK].astype(F32)
        return gathered(0, b).astype(F32)

    def half_cols(at, half):
        return pl.ds(pl.multiple_of(at * BLK + half * HALF, HALF), HALF)

    def u_part(layer, at, half):
        if layer == 0:
            return tokens[:, half_cols(at, half)].astype(F32)
        return ag_ref[0, half, at].astype(F32)

    def gain_part(layer, at, half):
        return gains[layer][pl.ds(2 * at + half, 1), :]

    def cot_block(layer, b):
        return cot[:, b * BLK : (b + 1) * BLK] if layer == 1 else gathered(1, b)

    def cot_part(layer, half):
        if layer == 1:
            return cot[:, half_cols(x, half)].astype(F32)
        return ag_ref[1, half, x].astype(F32)

    def wide_row(ref, at):
        return jnp.concatenate([ref[pl.ds(2 * at, 1), :], ref[pl.ds(2 * at + 1, 1), :]], axis=1)

    def indices():
        lane_lt = lax.broadcasted_iota(jnp.int32, (ROWS, ROWS), 0) < lax.broadcasted_iota(
            jnp.int32, (ROWS, ROWS), 1
        )
        tri = jnp.where(lane_lt, 1.0, 0.0).astype(BF16)
        slot = lax.broadcasted_iota(jnp.int32, (NT * SLOTS, ROWS), 0).astype(F32)
        dev = lax.broadcasted_iota(jnp.int32, (NT, ROWS), 0)
        lane = lax.broadcasted_iota(jnp.int32, (NT, ROWS), 1).astype(F32)
        own = wide_row(hpos, t) // ROWS
        hit = jnp.where(dev == own, 1.0, 0.0)
        before = dot(hit.astype(BF16), tri)
        send_id = jnp.sum(hit * (before + dev.astype(F32) * SLOTS), axis=0, keepdims=True)
        s = jnp.where(slot == send_id, 1.0, 0.0)
        s_ref[...] = s.astype(BF16)
        st_ref[...] = s.T.astype(BF16)
        every = jnp.concatenate([hpos[0::2, :], hpos[1::2, :]], axis=1)
        place = lax.rem(every, ROWS).astype(F32)
        mine = jnp.where(every // ROWS == t, 1.0, 0.0)
        rank = dot(mine.astype(BF16), tri)
        recv_id = jnp.zeros((1, ROWS), F32)
        for k in range(SLOTS):
            chosen = mine * jnp.where(rank == k, 1.0, 0.0)
            row = jnp.sum(chosen * (place + 1.0), axis=1, keepdims=True) - 1.0
            found = jnp.where(row == lane, dev.astype(F32) * SLOTS + k, 0.0)
            recv_id = recv_id + jnp.sum(found, axis=0, keepdims=True)
        r = jnp.where(slot == recv_id, 1.0, 0.0)
        rt_ref[...] = r.astype(BF16)
        r_ref[...] = r.T.astype(BF16)
        ids = wide_row(scene, t).astype(F32)
        for half, source in ((0, t), (1, mate)):
            row = wide_row(scene, source).astype(F32)
            col = jnp.broadcast_to(row, (128, ROWS)).T[:, :1]
            bias_ref[half] = jnp.where(col == ids, 0.0, -1e30)

    def normalize(layer):
        total = jnp.zeros((ROWS, 1), F32)
        for b in range(NX):
            ub = u_block(layer, b)
            total = total + jnp.sum(ub * ub, axis=1, keepdims=True)
        rinv = lax.rsqrt(total * (1.0 / (NX * BLK)) + EPS)
        rinv_ref[layer] = rinv
        for b in range(NX):
            hb = u_block(layer, b) * rinv * wide_row(gains[layer], b)
            h_ref[layer, :, b * BLK : (b + 1) * BLK] = hb.astype(BF16)

    def keys_values(layer):
        h = h_ref[layer]
        kv_ref[layer, 0, 0] = dot(h, qkvs[layer][1]).astype(BF16)
        kv_ref[layer, 0, 1] = dot(h, qkvs[layer][2]).astype(BF16)

    def send_kv(layer):
        return start(
            remote(kv_ref.at[layer, 0], kv_ref.at[layer, 1], KV + layer, {"tok": mate})
        )

    row_head = lax.broadcasted_iota(jnp.int32, (BLK, ROWS), 0) // HD
    lane_head = lax.broadcasted_iota(jnp.int32, (ROWS, BLK), 1) // HD

    def queries(layer):
        q = dot(h_ref[layer], qkvs[layer][0]).astype(BF16).astype(F32) * 0.125
        q_ref[layer] = q.astype(BF16)
        qt = q.T
        for n in range(HEADS):
            qt_ref[:, n * ROWS : (n + 1) * ROWS] = jnp.where(row_head == n, qt, 0.0).astype(BF16)

    def attend(layer):
        for half in range(2):
            kt_ref[layer, half] = kv_ref[layer, half, 0].T
            vt_ref[layer, half] = kv_ref[layer, half, 1].T
        for n in range(HEADS):
            cols = slice(n * ROWS, (n + 1) * ROWS)
            rows = slice(n * HD, (n + 1) * HD)
            e = []
            for half in range(2):
                scores = dot(kv_ref[layer, half, 0], qt_ref[:, cols])
                if layer == 1:
                    scores = scores + bias_ref[half]
                e.append(jnp.exp(scores))
            total = jnp.sum(e[0], axis=0, keepdims=True) + jnp.sum(e[1], axis=0, keepdims=True)
            inv = 1.0 / total
            mixed = jnp.zeros((HD, ROWS), F32)
            for half in range(2):
                p = e[half] * inv
                p_ref[layer, half, :, cols] = p
                pb = p.astype(BF16)
                pb_ref[layer, half, :, cols] = pb
                mixed = mixed + dot(vt_ref[layer, half, rows, :], pb)
            obt_ref[rows, :] = mixed.astype(BF16)
        ob_ref[layer] = obt_ref[...].T

    def turn_h(layer):
        for b in range(NX):
            ht_ref[layer, b * BLK : (b + 1) * BLK, :] = h_ref[layer, :, b * BLK : (b + 1) * BLK].T

    def pull_back_out(layer):
        acc = jnp.zeros((ROWS, BLK), F32)
        for b in range(NX):
            acc = acc + dot_nt(cot_block(layer, b), outs[layer][:, b * BLK : (b + 1) * BLK])
        do = acc.astype(BF16)
        do_ref[...] = do
        dot_ref[...] = do.T
        for n in range(HEADS):
            dostk_ref[n * ROWS : (n + 1) * ROWS, :] = jnp.where(
                lane_head == n, do.astype(F32), 0.0
            ).astype(BF16)

    def attend_back(layer, meanwhile):
        q = q_ref[layer].astype(F32)
        dt = dot_ref[...].astype(F32)
        for n in range(HEADS):
            cols = slice(n * ROWS, (n + 1) * ROWS)
            rows = slice(n * HD, (n + 1) * HD)
            qstk_ref[n * ROWS : (n + 1) * ROWS, :] = jnp.where(lane_head == n, q, 0.0).astype(BF16)
            only = jnp.where(row_head == n, dt, 0.0).astype(BF16)
            dp = [dot(kv_ref[layer, half, 1], only) for half in range(2)]
            p = [p_ref[layer, half, :, cols] for half in range(2)]
            r = jnp.sum(dp[0] * p[0], axis=0, keepdims=True) + jnp.sum(
                dp[1] * p[1], axis=0, keepdims=True
            )
            dq = jnp.zeros((HD, ROWS), F32)
            for half in range(2):
                ds = (p[half] * (dp[half] - r)).astype(BF16)
                ds_ref[half, :, cols] = ds
                dq = dq + dot(kt_ref[layer, half, rows, :], ds)
            dqt_ref[rows, :] = (dq * 0.125).astype(BF16)
        kvs_ref[layer, 0] = dot(ds_ref[1], qstk_ref[...]).astype(BF16)
        kvs_ref[layer, 1] = dot(pb_ref[layer, 1], dostk_ref[...]).astype(BF16)
        copy = start(
            remote(kvs_ref.at[layer], kvr_ref.at[layer], BACK + layer, {"tok": mate})
        )
        dqkv_ref[0] = dqt_ref[...].T
        dk = dot(ds_ref[0], qstk_ref[...])
        dv = dot(pb_ref[layer, 0], dostk_ref[...])
        meanwhile()
        copy.wait_recv()
        dqkv_ref[1] = (dk + kvr_ref[layer, 0].astype(F32)).astype(BF16)
        dqkv_ref[2] = (dv + kvr_ref[layer, 1].astype(F32)).astype(BF16)

    def dh_part(layer, at, half):
        rows = half_cols(at, half)
        acc = dot_nt(dqkv_ref[0], qkvs[layer][0, rows, :])
        acc = acc + dot_nt(dqkv_ref[1], qkvs[layer][1, rows, :])
        return acc + dot_nt(dqkv_ref[2], qkvs[layer][2, rows, :])

    def send_part(phase, half, j, part):
        rss_ref[phase, half, j] = part.astype(BF16)
        sem = RS + 8 * phase + 4 * half + j
        return start(remote(rss_ref.at[phase, half, j], rsr_ref.at[phase, half, j], sem, xdev(j)))

    def send_dh(layer):
        phase = 2 - layer
        sums = jnp.zeros((ROWS, 1), F32)
        copies = ([], [])
        own = [None, None]
        rinv = rinv_ref[layer]
        for half in range(2):
            for j in (2, 1, 3, 0):
                at = lax.rem(x + j, NX)
                part = dh_part(layer, at, half)
                if j:
                    copies[half].append(send_part(phase, half, j, part))
                else:
                    own[half] = part
                weighted = part * u_part(layer, at, half)
                sums = sums + jnp.sum(
                    weighted * gain_part(layer, at, half), axis=1, keepdims=True
                )
                n0_ref[at, layer : layer + 1, half * HALF : (half + 1) * HALF] = jnp.sum(
                    weighted * rinv, axis=0, keepdims=True
                )
        ms_ref[layer] = jnp.broadcast_to(sums, (ROWS, 128)).T[:8, :]
        for j in (2, 1, 3):
            sem = ROWSUM + 4 * layer + j
            copies[0].append(start(remote(ms_ref.at[layer], mr_ref.at[layer, j], sem, xdev(j))))
        return own, copies

    def row_mean(layer):
        sums = ms_ref[layer]
        for j in range(1, NX):
            sums = sums + mr_ref[layer, j]
        return jnp.broadcast_to(sums[:1, :], (128, ROWS)).T[:, :1] * (1.0 / (NX * BLK))

    def wait_all(copies):
        for copy in copies:
            copy.wait_recv()

    def total_part(phase, half, own):
        for j in range(1, NX):
            own = own + rsr_ref[phase, half, j].astype(F32)
        return own

    def finish_dh(layer, half, dh, mean):
        u = u_part(layer, x, half)
        rinv = rinv_ref[layer]
        scaled = dh * gain_part(layer, x, half)
        du = cot_part(layer, half) + rinv * (scaled - u * rinv * rinv * mean)
        return du.astype(BF16)

    def relay_out(way, half, table, chunk):
        packed = dot(table[...], chunk).reshape(NT, SLOTS, HALF)
        as_ref[way, half] = packed.astype(BF16)
        ar_ref[way, half, t] = as_ref[way, half, t]
        sem = A2A + 2 * way + half

        to_y = {dy: lax.rem(y + dy, NY) for dy in (2, 1, 3, 0)}
        to_z = {dz: lax.rem(z + dz, NZ) for dz in (4, 3, 5, 2, 6, 1, 7, 0)}
        for dy in to_y:
            for dz in to_z:
                for dc in (1, 0):
                    if dy or dz or dc:
                        to = (to_y[dy] * NZ + to_z[dz]) * 2 + (core if dc == 0 else 1 - core)
                        place = ar_ref.at[way, half, t]
                        remote(as_ref.at[way, half, to], place, sem, {"tok": to}).start()
        every = pl.ds(0, NT - 1)
        copy = remote(
            as_ref.at[way, half, every], ar_ref.at[way, half, every], sem, {"tok": mate}
        )
        sends.append(copy)
        return copy

    def relay_in(way, half, table, copy):
        copy.wait_recv()
        packed = ar_ref[way, half].astype(F32).reshape(NT * SLOTS, HALF).astype(BF16)
        return dot(table[...], packed).astype(BF16)

    def spread(phase, half, chunk):
        ag_ref[phase, half, x] = chunk
        place = ag_ref.at[phase, half, x]
        sem = AG + 8 * phase + 4 * half
        return [start(remote(place, place, sem + j, xdev(j))) for j in (2, 1, 3)]

    def turn_cot():
        for half in range(2):
            for b in range(NX):
                at = b * BLK + half * HALF
                ct_ref[half, b * HALF : (b + 1) * HALF, :] = cot[:, at : at + HALF].T

    def put_grad(layer, kind, chip, value):
        n = value.shape[0] // 32
        pieces = value.reshape(n, 2, 16, BLK)
        for c in range(2):
            g_ref[layer, c, chip : chip + n, kind * 16 : (kind + 1) * 16, :] = pieces[:, c].astype(
                BF16
            )

    def out_grads(layer, half):
        for b in range(NX):
            if layer == 0:
                left = ag_ref[1, half, b].T
            else:
                left = ct_ref[half, b * HALF : (b + 1) * HALF, :]
            put_grad(layer, 0, b * NZ + half * (NZ // 2), dot(left, ob_ref[layer]))

    def qkv_grads(layer, kinds):
        for b in range(NX):
            left = ht_ref[layer, b * BLK : (b + 1) * BLK, :]
            for kind in kinds:
                put_grad(layer, kind + 1, b * NZ, dot(left, dqkv_ref[kind]))

    def rows_of(layer, group):
        first, count = GROUPS[group]
        return pl.ds(first, count)

    def grads_core(layer, group):
        rows = rows_of(layer, group)
        return start(
            remote(
                g_ref.at[layer, 1 - core, :, rows],
                gc_ref.at[layer, :, rows],
                GC + 3 * layer + group,
                {"tok": mate},
            )
        )

    def grads_y(layer, group, copy):
        copy.wait_recv()
        rows = rows_of(layer, group)
        sem = GY + 12 * layer + 4 * group
        copies = []
        for j in (2, 1, 3, 0):
            chips = pl.ds(lax.rem(y + j, NY) * NZ, NZ)
            value = g_ref[layer, core, chips, rows].astype(F32)
            value = value + gc_ref[layer, chips, rows].astype(F32)
            g2_ref[layer, j, :, rows] = value.astype(BF16)
            if j:
                place = g2_ref.at[layer, j, :, rows]
                copies.append(
                    start(remote(place, gy_ref.at[layer, j, :, rows], sem + j, ydev(j)))
                )
        return copies

    def grads_z(layer, group, copies):
        wait_all(copies)
        rows = rows_of(layer, group)
        sem = GZ + 24 * layer + 8 * group
        later = []
        for j in (4, 3, 5, 2, 6, 1, 7, 0):
            at = lax.rem(z + j, NZ)
            value = g2_ref[layer, 0, at, rows].astype(F32)
            for k in range(1, NY):
                value = value + gy_ref[layer, k, at, rows].astype(F32)
            g3_ref[layer, j, rows] = value.astype(BF16)
            if j:
                place = g3_ref.at[layer, j, rows]
                later.append(start(remote(place, gz_ref.at[layer, j, rows], sem + j, zdev(j))))
        return later

    def grads_end(layer, group, copies):
        wait_all(copies)
        rows = rows_of(layer, group)
        value = g3_ref[layer, 0, rows].astype(F32)
        for j in range(1, NZ):
            value = value + gz_ref[layer, j, rows].astype(F32)
        value = value * GRAD_SCALE
        o_qkv = (o_qkv1, o_qkv2)[layer]
        first, count = GROUPS[group]
        for i in range(count // 16):
            o_qkv[first // 16 + i - 1] = value[i * 16 : (i + 1) * 16, :]

    def out_z(layer, copy):
        copy.wait_recv()
        copies = []
        for j in (4, 3, 5, 2, 6, 1, 7, 0):
            at = lax.rem(z + j, NZ)
            for k in range(NY):
                chip = k * NZ + at
                value = g_ref[layer, core, chip, 0:16].astype(F32)
                value = value + gc_ref[layer, chip, 0:16].astype(F32)
                e2_ref[layer, j, k] = value.astype(BF16)
            if j:
                place = e2_ref.at[layer, j]
                copies.append(
                    start(remote(place, ez_ref.at[layer, j], GZ + 24 * layer + j, zdev(j)))
                )
        return copies

    def out_y(layer, copies):
        wait_all(copies)
        later = []
        for j in (2, 1, 3, 0):
            at = lax.rem(y + j, NY)
            value = e2_ref[layer, 0, at].astype(F32)
            for k in range(1, NZ):
                value = value + ez_ref[layer, k, at].astype(F32)
            e3_ref[layer, j] = value.astype(BF16)
            if j:
                place = e3_ref.at[layer, j]
                later.append(
                    start(remote(place, ey_ref.at[layer, j], GY + 12 * layer + j, ydev(j)))
                )
        return later

    def out_end(layer, copies):
        wait_all(copies)
        value = e3_ref[layer, 0].astype(F32)
        for j in range(1, NY):
            value = value + ey_ref[layer, j].astype(F32)
        (o_out1, o_out2)[layer][...] = value * GRAD_SCALE

    def hop_one(layer, group, copy):
        return grads_y(layer, group, copy) if group else out_z(layer, copy)

    def hop_two(layer, group, copies):
        return grads_z(layer, group, copies) if group else out_y(layer, copies)

    def hops_end(layer, group, copies):
        if group:
            grads_end(layer, group, copies)
        else:
            out_end(layer, copies)

    loads[0].wait()
    normalize(0)
    loads[1].wait()
    loads[2].start()
    keys_values(0)
    queries(0)
    pl.semaphore_wait(barrier, len(near))
    kv_copy = send_kv(0)
    for j in range(1, NY):
        pl.semaphore_signal(y_known, inc=1, device_id=ydev(j), device_id_type=MESH)
    turn_h(0)
    n0_ref[...] = jnp.zeros_like(n0_ref)
    kv_copy.wait_recv()
    for load in loads[3:]:
        load.start()
    attend(0)
    loads[2].wait()
    copies = ([], [])
    own = [None, None]
    for half in range(2):
        for j in (2, 1, 3, 0):
            part = dot(ob_ref[0], out1[:, half_cols(lax.rem(x + j, NX), half)])
            if j:
                copies[half].append(send_part(0, half, j, part))
            else:
                own[half] = part
    pl.semaphore_wait(y_known, NY - 1)
    pl.semaphore_signal(all_known, inc=1, device_id={"tok": mate}, device_id_type=MESH)
    indices()
    pl.semaphore_wait(all_known, 1)
    relays = []
    for half in range(2):
        wait_all(copies[half])
        y1 = (u_part(0, x, half) + total_part(0, half, own[half])).astype(BF16)
        relays.append(relay_out(0, half, s_ref, y1))
    for load in loads[3:]:
        load.wait()
    pull_back_out(1)
    turn_cot()
    copies = []
    for half in range(2):
        copies += spread(0, half, relay_in(0, half, r_ref, relays[half]))
    wait_all(copies)

    normalize(1)
    keys_values(1)
    kv_copy = send_kv(1)
    queries(1)
    turn_h(1)
    kv_copy.wait_recv()
    attend(1)
    cores_two = []

    def meanwhile_two():
        for half in range(2):
            out_grads(1, half)
        cores_two.append(grads_core(1, 0))

    attend_back(1, meanwhile_two)
    own, copies = send_dh(1)
    qkv_grads(1, (0,))
    cores_two.append(grads_core(1, 1))
    ys_two = [hop_one(1, 0, cores_two[0])]
    qkv_grads(1, (1, 2))
    cores_two.append(grads_core(1, 2))
    ys_two.append(hop_one(1, 1, cores_two[1]))
    relays = []
    for half in range(2):
        wait_all(copies[half])
        if half == 0:
            mean = row_mean(1)
        du2 = finish_dh(1, half, total_part(1, half, own[half]), mean)
        relays.append(relay_out(1, half, rt_ref, du2))
    copies = []
    for half in range(2):
        copies.append(spread(1, half, relay_in(1, half, st_ref, relays[half])))
    ys_two.append(hop_one(1, 2, cores_two[2]))
    zs_two = [hop_two(1, group, ys_two[group]) for group in range(2)]

    for half in range(2):
        wait_all(copies[half])
        out_grads(0, half)
    cores_one = [grads_core(0, 0)]
    pull_back_out(0)
    ys_one = []

    def meanwhile_one():
        qkv_grads(0, (0,))
        cores_one.append(grads_core(0, 1))
        ys_one.append(hop_one(0, 0, cores_one[0]))

    attend_back(0, meanwhile_one)
    qkv_grads(0, (1, 2))
    cores_one.append(grads_core(0, 2))
    ys_one.append(hop_one(0, 1, cores_one[1]))
    zs_two.append(hop_two(1, 2, ys_two[2]))
    own, copies = send_dh(0)
    gain_copies = [start(remote(n0_ref, nc_ref, NC, {"tok": mate}))]
    ys_one.append(hop_one(0, 2, cores_one[2]))
    wait_all(gain_copies)
    n1_ref[...] = n0_ref[...] + nc_ref[...]
    gain_copies = [
        start(remote(n1_ref.at[lax.rem(y + j, NY)], ny_ref.at[j], NYS + j, ydev(j)))
        for j in range(1, NY)
    ]
    for group in range(3):
        hops_end(1, group, zs_two[group])
    zs_one = [hop_two(0, group, ys_one[group]) for group in range(2)]
    gathers = []
    for half in range(2):
        wait_all(copies[half])
        if half == 0:
            mean = row_mean(0)
        gathers += spread(2, half, finish_dh(0, half, total_part(2, half, own[half]), mean))
    wait_all(gain_copies)
    n2_ref[...] = n1_ref[y] + ny_ref[1] + ny_ref[2] + ny_ref[3]
    gain_copies = [start(remote(n2_ref, nz_ref.at[j], NZS + j, zdev(j))) for j in range(1, NZ)]
    zs_one.append(hop_two(0, 2, ys_one[2]))
    wait_all(gain_copies)
    value = n2_ref[...]
    for j in range(1, NZ):
        value = value + nz_ref[j]
    n3_ref[...] = value
    gain_copies = [start(remote(n3_ref, nx_ref.at[j], NXS + j, xdev(j))) for j in range(1, NX)]
    wait_all(gathers)
    for b in range(NX):
        o_gin[:, b * BLK : (b + 1) * BLK] = gathered(2, b)
    wait_all(gain_copies)
    o_gain[...] = (n3_ref[...] + nx_ref[1] + nx_ref[2] + nx_ref[3]) * GRAD_SCALE
    for group in range(3):
        hops_end(0, group, zs_one[group])
    for copy in sends:
        copy.wait_send()


def deliver(
    gin, qkv1, out1, qkv2, out2, gains, o_gin, o_qkv1, o_out1, o_gain1, o_qkv2, o_out2, o_gain2
):
    pairs = ((gin, o_gin), (qkv1, o_qkv1), (out1, o_out1), (qkv2, o_qkv2), (out2, o_out2))
    for a, b in pairs:
        b[...] = a[...]
    at = lax.rem(lax.axis_index("tok"), NT // NX) * 16
    mine = pltpu.roll(gains[...], lax.rem(BLK - at, BLK), 1)
    o_gain1[...] = mine[0, :16]
    o_gain2[...] = mine[1, :16]


def scratch():
    def b16(*shape):
        return pltpu.VMEM(shape, BF16)

    def f32(*shape):
        return pltpu.VMEM(shape, F32)

    wide = NT * SLOTS
    width = NX * BLK
    return [
        b16(ROWS, width), b16(3, width, BLK), b16(BLK, width),
        b16(3, width, BLK), b16(BLK, width), b16(ROWS, width),
        b16(wide, ROWS), b16(ROWS, wide), b16(ROWS, wide), b16(wide, ROWS), f32(2, ROWS, ROWS),
        b16(2, ROWS, NX * BLK), b16(2, NX * BLK, ROWS), f32(2, ROWS, 1),
        b16(2, 2, 2, ROWS, BLK), b16(2, 2, BLK, ROWS), b16(2, 2, BLK, ROWS),
        b16(2, ROWS, BLK), b16(BLK, HEADS * ROWS), f32(2, 2, ROWS, HEADS * ROWS),
        b16(2, 2, ROWS, HEADS * ROWS), b16(BLK, ROWS), b16(2, ROWS, BLK),
        b16(ROWS, BLK), b16(BLK, ROWS), b16(2, ROWS, HEADS * ROWS), b16(HEADS * ROWS, BLK),
        b16(HEADS * ROWS, BLK), b16(BLK, ROWS), b16(3, ROWS, BLK), b16(2, 2, ROWS, BLK),
        b16(2, 2, ROWS, BLK), b16(2, NX * HALF, ROWS),
        b16(3, 2, NX, ROWS, HALF), b16(3, 2, NX, ROWS, HALF), f32(2, 8, ROWS), f32(2, NX, 8, ROWS),
        b16(2, 2, NT, SLOTS, HALF), b16(2, 2, NT, SLOTS, HALF), b16(3, 2, NX, ROWS, HALF),
        b16(2, 2, NY * NZ, 64, BLK), b16(2, NY * NZ, 64, BLK), b16(2, NY, NZ, 64, BLK),
        b16(2, NY, NZ, 64, BLK), b16(2, NZ, 64, BLK), b16(2, NZ, 64, BLK),
        b16(2, NZ, NY, 16, BLK), b16(2, NZ, NY, 16, BLK), b16(2, NY, 16, BLK), b16(2, NY, 16, BLK),
        f32(NX, 8, BLK), f32(NX, 8, BLK), f32(NX, 8, BLK), f32(NY, 8, BLK), f32(8, BLK),
        f32(NZ, 8, BLK), f32(8, BLK), f32(NX, 8, BLK),
        pltpu.SemaphoreType.DMA((NSEM,)), pltpu.SemaphoreType.DMA((NSEM,)),
        pltpu.SemaphoreType.DMA((6,)), pltpu.SemaphoreType.REGULAR, pltpu.SemaphoreType.REGULAR,
    ]


def local(
    tokens, gain_one, qkv_one, out_one, gain_two, qkv_two, out_two, hilbert_pos, scene, cotangent
):
    vmem = pl.BlockSpec(memory_space=pltpu.VMEM)
    hbm = pl.BlockSpec(memory_space=pl.ANY)
    grads = [
        jax.ShapeDtypeStruct((3, 16, BLK), F32),
        jax.ShapeDtypeStruct((16, BLK), F32),
    ]
    grad_input, qkv1, out1, qkv2, out2, gains = pl.pallas_call(
        kernel,
        out_shape=[
            jax.ShapeDtypeStruct((ROWS, NX * BLK), BF16),
            *grads,
            *grads,
            jax.ShapeDtypeStruct((8, BLK), F32),
        ],
        in_specs=[hbm, vmem, hbm, hbm, vmem, hbm, hbm, vmem, vmem, hbm],
        out_specs=[vmem] * 6,
        scratch_shapes=scratch(),
        compiler_params=pltpu.CompilerParams(
            collective_id=0, has_side_effects=True, vmem_limit_bytes=58 * 2**20
        ),
    )(
        tokens,
        gain_one.reshape(2 * NX, 128),
        qkv_one,
        out_one,
        gain_two.reshape(2 * NX, 128),
        qkv_two,
        out_two,
        hilbert_pos.reshape(2 * NT, 128),
        scene.reshape(2 * NT, 128),
        cotangent,
    )
    small = jax.ShapeDtypeStruct((16,), F32)
    grad_input, qkv1, out1, gain1, qkv2, out2, gain2 = pl.pallas_call(
        deliver,
        out_shape=[
            jax.ShapeDtypeStruct((ROWS, NX * BLK), BF16),
            *grads,
            small,
            *grads,
            small,
        ],
        in_specs=[vmem] * 6,
        out_specs=[vmem] * 7,
    )(grad_input, qkv1, out1, qkv2, out2, gains)
    return grad_input, qkv1, out1, gain1, qkv2, out2, gain2


def solution(mesh):
    in_specs = (
        P("tok", None),
        P(),
        P(None, None, "head"),
        P("head", None),
        P(),
        P(None, None, "head"),
        P("head", None),
        P(),
        P(),
        P("tok", None),
    )
    out_specs = (
        P("tok", None),
        P(None, "tok", "head"),
        P("tok", "head"),
        P("tok"),
        P(None, "tok", "head"),
        P("tok", "head"),
        P("tok"),
    )
    return jax.shard_map(local, mesh=mesh, in_specs=in_specs, out_specs=out_specs, check_vma=False)
```
